128 devices in a mesh: fsdp: 128 (over y, x, z, core).
Axes of the slice: x: 4, y: 4, z: 4, core: 2. Of those that a mesh axis runs over, the one named last changes fastest.
Arguments:
- tokens: bfloat16 [32768, 1024], P('fsdp'), may hold values from -6 to 6
- sequence_lengths: int32 [128, 4], P('fsdp'), may hold values from 0 to 256, as said below
- expert_index: int32 [32768, 8], P('fsdp'), may hold values from 0 to 11, all different within a row; in each aligned block of 256 rows (0 to 255, 256 to 511, ...) at most 203 rows name the same one
- cotangent: bfloat16 [32768, 1024], P('fsdp'), may hold values from -24 to 24
- query_weight: bfloat16 [1024, 1024], P('fsdp'), may hold values from -0.25 to 0.25
- key_weight: bfloat16 [1024, 512], P('fsdp'), may hold values from -0.25 to 0.25
- value_weight: bfloat16 [1024, 512], P('fsdp'), may hold values from -0.1875 to 0.1875
- output_weight: bfloat16 [1024, 1024], P('fsdp'), may hold values from -0.75 to 0.75
- attention_gain: bfloat16 [1024], P('fsdp'), may hold values from 0.25 to 1.75
- router_weight: bfloat16 [1024, 12], P('fsdp'), may hold values from -0.09375 to 0.09375
- mixture_gain: bfloat16 [1024], P('fsdp'), may hold values from 0.25 to 1.75
- gate_weight: bfloat16 [12, 1024, 512], P(None, 'fsdp'), may hold values from -0.1875 to 0.1875
- up_weight: bfloat16 [12, 1024, 512], P(None, 'fsdp'), may hold values from -0.1875 to 0.1875
- down_weight: bfloat16 [12, 512, 1024], P(None, 'fsdp'), may hold values from -0.75 to 0.75
Outputs:
- layer_out: bfloat16 [32768, 1024], P('fsdp')
- grad_tokens: bfloat16 [32768, 1024], P('fsdp')
- query_grad: float32 [1024, 1024], P('fsdp')
- key_grad: float32 [1024, 512], P('fsdp')
- value_grad: float32 [1024, 512], P('fsdp')
- output_grad: float32 [1024, 1024], P('fsdp')
- attention_gain_grad: float32 [1024], P('fsdp')
- router_grad: float32 [1024, 12], P('fsdp')
- mixture_gain_grad: float32 [1024], P('fsdp')
- gate_grad: float32 [12, 1024, 512], P(None, 'fsdp')
- up_grad: float32 [12, 1024, 512], P(None, 'fsdp')
- down_grad: float32 [12, 512, 1024], P(None, 'fsdp')
The draws below stay inside these ranges and needn't reach their ends.
Inputs may be any that keep to these rules, and one draw needn't show every extreme that they name: `sequence_lengths`: row b lists the sequences of block b in order from its first row; they sum to at most 256, and in every draw some block holds a single sequence of 256 rows. `expert_index`: each row names 8 different experts. No expert is named by more than 203 rows of one block of 256 rows, a bound that some block reaches.
All inputs are finite; a program needn't handle non-finite values.
Results may differ from the reference program's by a relative error of at most 0.015.
The reference program's roundings to bfloat16 on the way count: a program that leaves them out, or rounds other values in their place, can miss the bound.
Values may be sent and summed in bfloat16 or wider, within the bound.
No kernel may reach another device: no remote copies, remote signals or barrier semaphores. Data moves between devices by JAX's collectives and lax.ppermute only.
A program may use at most 384 MiB of HBM per device.

```python
import math
import jax
import jax.numpy as jnp
import numpy as np
from jax import lax

D = 1024
HEADS = 16
KV_HEADS = 8
HEAD_DIM = 64
FF = 512
EXPERTS = 12
TOP = 8
SEQ_DEV = 4
TOK_DEV = 256
CAP = 203
TOKENS = 32768
N_FSDP = 128


def draw_sequence_lengths(key, part):
    key = jax.random.fold_in(key, 7)
    subkeys = jax.random.split(key, 3)
    totals = jax.random.randint(subkeys[0], (N_FSDP, 1), TOK_DEV // 2, TOK_DEV + 1)
    cut_points = jax.random.randint(subkeys[1], (N_FSDP, SEQ_DEV - 1), 0, TOK_DEV + 1)
    cut_points = jnp.sort(jnp.minimum(cut_points, totals), axis=1)
    boundaries = jnp.concatenate([jnp.zeros((N_FSDP, 1), jnp.int32), cut_points, totals], axis=1)
    lengths = boundaries[:, 1:] - boundaries[:, :-1]
    chosen = jax.random.randint(subkeys[2], (), 0, N_FSDP)
    full_row = jnp.zeros((SEQ_DEV,), jnp.int32).at[0].set(TOK_DEV)
    lengths = jnp.where((jnp.arange(N_FSDP) == chosen)[:, None], full_row[None, :], lengths)
    return lengths.astype(jnp.int32)


def with_spikes(result, rng, source, target, blocks, factor):
    def block_of(dim):
        return (jnp.arange(result.shape[dim]) // (result.shape[dim] // blocks)).reshape((-1,) + (1,) * (result.ndim - 1 - dim))

    first = jax.random.permutation(rng, blocks)[block_of(target)]
    second = (block_of(target) + blocks // 2) % blocks
    return jnp.where((block_of(source) == first) | (block_of(source) == second), factor * result, result)


def block_scale(own_key, extent, cuts, smallest, top_value):
    level = 1.0
    for axis_at, blocks in cuts:
        draws = jax.random.uniform(jax.random.fold_in(jax.random.fold_in(own_key, 6), axis_at), (blocks,), jnp.float32, smallest / len(cuts), top_value / len(cuts))
        level = level * jnp.repeat(jnp.exp(draws), extent[axis_at] // blocks).reshape((-1,) + (1,) * (len(extent) - 1 - axis_at))
    return level


def routed_block(key, own, number, rows, count, top, bound, lean):
    sequence = jax.random.permutation(key, count)
    heavy_load, ordinary = shares(count, rows * top, bound, lean, True), shares(count, rows * top, bound, lean, False)
    places = jnp.arange(count)

    def named(sizes, rotation):
        used = int((sizes > 0).sum())
        fixed = max(1, used // 4)
        passed = fixed + (places - fixed + rotation * (used - fixed)) % max(1, count - fixed)
        return jnp.zeros((count,), jnp.int32).at[sequence[jnp.where(places < fixed, places, passed)]].set(jnp.asarray(sizes, jnp.int32))

    sizes = jnp.where(number % 4 == 0, named(heavy_load, number // 4), named(ordinary, number - number // 4 - 1))
    mixed = jax.random.permutation(jax.random.fold_in(own, 3), count)
    source_of, sink = mixed[0:count // 2 * 2:2], mixed[1:count // 2 * 2:2]
    room = jnp.minimum(sizes[source_of] - 1, bound - sizes[sink]) // 2
    room = jnp.where((source_of == sequence[0]) | (sink == sequence[0]) | (sizes[sink] == 0), 0, jnp.maximum(room, 0))
    passed = jax.random.randint(jax.random.fold_in(own, 4), (count // 2,), 0, 1 << 20) % (room + 1)
    sizes = sizes.at[source_of].add(-passed).at[sink].add(passed)
    members = jnp.searchsorted(jnp.cumsum(sizes), jnp.arange(rows * top), side="right").astype(jnp.int32)
    table = members.reshape(top, rows).T
    table = table[jax.random.permutation(jax.random.fold_in(own, 1), rows)]
    rotation = jax.random.randint(jax.random.fold_in(own, 2), (rows, 1), 0, top)
    return jnp.take_along_axis(table, (jnp.arange(top)[None, :] + rotation) % top, axis=1)


def shares(amount, total, reach, lean, full):
    weights = [(1 << 20) // math.isqrt(rank ** lean) + 1 for rank in range(1, amount + 1)]
    largest = reach if full else min(reach, max(-(-total // amount), total * weights[0] // sum(weights)))
    least = 1 if total - largest >= amount - 1 else 0
    holding, surplus = [largest] + [least] * (amount - 1), total - largest - least * (amount - 1)
    while surplus > 0:
        candidates = [i for i in range(1, amount) if holding[i] < largest] or [i for i in range(1, amount) if holding[i] < reach]
        pool, left = sum([weights[i] for i in candidates]), surplus
        for i in candidates:
            more = min(reach - holding[i], max(1, left * weights[i] // pool), surplus)
            holding[i] = holding[i] + more
            surplus = surplus - more
    return np.array(holding)


def scatter_about(rng, dims, deviation, limit, shards=(), held_as=jnp.bfloat16):
    entries = jax.random.normal(rng, dims, jnp.float32) * deviation
    if len(shards) > 0:
        entries = block_scale(rng, dims, shards, -0.22, 0.18) * entries
    return jnp.clip(entries, min=-limit, max=limit).astype(held_as)


def bell_draw_with(stream_key, shape, width, limit, cuts, heavy, kind=jnp.bfloat16):
    array = width * jax.random.normal(stream_key, shape, jnp.float32)
    if cuts:
        array = array * block_scale(stream_key, shape, cuts, -0.22, 0.18)
    return jnp.clip(with_spikes(array, jax.random.fold_in(stream_key, 3), *heavy), -limit, limit).astype(kind)


def setup_inputs(seed: int = 0) -> dict:
    key_of = jax.random.split(jax.random.key(seed), 15)
    tokens = scatter_about(key_of[0], (TOKENS, D), 1.0, 6.0, ((0, 128),))
    sequence_lengths = draw_sequence_lengths(jax.random.fold_in(key_of[14], 71), 0)
    expert_index_keys = jax.random.split(jax.random.fold_in(key_of[2], 1), TOKENS // TOK_DEV)
    expert_index_turns = jax.random.permutation(jax.random.fold_in(key_of[2], 3), TOKENS // TOK_DEV)
    expert_index = jax.vmap(lambda own, number: routed_block(jax.random.fold_in(key_of[2], 2), own, number, TOK_DEV, EXPERTS, TOP, CAP, 0))(expert_index_keys, expert_index_turns).reshape((TOKENS, TOP))
    cotangent = bell_draw_with(key_of[3], (TOKENS, D), 1.0, 24.0, ((0, 128),), (0, 1, 128, 5.5))
    query_weight = scatter_about(key_of[4], (D, HEADS * HEAD_DIM), (D // 2) ** -0.5, 0.25, ((0, 128),))
    key_weight = scatter_about(key_of[5], (D, KV_HEADS * HEAD_DIM), (D // 2) ** -0.5, 0.25, ((0, 128),))
    value_weight = scatter_about(key_of[6], (D, KV_HEADS * HEAD_DIM), D ** -0.5, 0.1875, ((0, 128),))
    output_weight = scatter_about(key_of[7], (HEADS * HEAD_DIM, D), (HEADS * HEAD_DIM // 16) ** -0.5, 0.75, ((0, 128),))
    attention_gain = jnp.clip(1.0 + 0.15 * jax.random.normal(key_of[8], (D,), jnp.float32), 0.25, 1.75).astype(jnp.bfloat16)
    router_weight = scatter_about(key_of[9], (D, EXPERTS), (4 * D) ** -0.5, 0.09375, ((0, 128),))
    mixture_gain = jnp.clip(1.0 + 0.15 * jax.random.normal(key_of[10], (D,), jnp.float32), 0.25, 1.75).astype(jnp.bfloat16)
    gate_weight = scatter_about(key_of[11], (EXPERTS, D, FF), D ** -0.5, 0.1875, ((1, 128),))
    up_weight = scatter_about(key_of[12], (EXPERTS, D, FF), D ** -0.5, 0.1875, ((1, 128),))
    down_weight = scatter_about(key_of[13], (EXPERTS, FF, D), (FF // 8) ** -0.5, 0.75, ((1, 128),))
    return {"tokens": tokens, "sequence_lengths": sequence_lengths, "expert_index": expert_index, "cotangent": cotangent, "query_weight": query_weight, "key_weight": key_weight, "value_weight": value_weight, "output_weight": output_weight, "attention_gain": attention_gain, "router_weight": router_weight, "mixture_gain": mixture_gain, "gate_weight": gate_weight, "up_weight": up_weight, "down_weight": down_weight}


@jax.custom_vjp
def low(v):
    return lax.optimization_barrier(v.astype(jnp.bfloat16)).astype(jnp.float32)

@jax.custom_vjp
def low_back(v):
    return v

def low_keep(v):
    return (low(v), None)

def low_pass(kept, grad):
    return (grad,)

def back_keep(v):
    return (v, None)

def back_low(kept, grad):
    return (low(grad),)
low.defvjp(low_keep, low_pass)
low_back.defvjp(back_keep, back_low)
epsilon = 1e-06
rope_base = 10000.0

def matmul(left_side, right_side):
    return jnp.dot(left_side, right_side, precision=lax.Precision.HIGHEST)

def rms_scale(activations):
    return lax.rsqrt(lax.optimization_barrier(jnp.mean(activations * activations, axis=1, keepdims=True)) + epsilon)

def seq_layout(lengths):
    ends_at = jnp.cumsum(lengths).astype(jnp.int32)
    starts_at = (ends_at - lengths).astype(jnp.int32)
    slot_index = jnp.arange(TOK_DEV, dtype=jnp.int32)
    segment = lax.optimization_barrier(jnp.sum((slot_index[:, None] >= ends_at[None, :]).astype(jnp.int32), axis=1))
    owners = segment[:, None] == jnp.arange(SEQ_DEV, dtype=jnp.int32)[None, :]
    begins = lax.optimization_barrier(jnp.sum(jnp.where(owners, starts_at[None, :], 0), axis=1)).astype(jnp.int32)
    return (segment, slot_index - begins, segment < SEQ_DEV)

def rope_tables(position):
    half_size = HEAD_DIM // 2
    frequency = rope_base ** (-2.0 * jnp.arange(half_size, dtype=jnp.float32) / HEAD_DIM)
    angles = position.astype(jnp.float32)[:, None] * frequency[None, :]
    return (jnp.cos(angles)[:, None, :], jnp.sin(angles)[:, None, :])

def rotate(operand, cosine, sine_part):
    half_size = operand.shape[-1] // 2
    first_half = operand[..., :half_size]
    second_half = operand[..., half_size:]
    return jnp.concatenate([first_half * cosine - second_half * sine_part, second_half * cosine + first_half * sine_part], axis=-1)

def layer_block(params, token_block, length_block, index_block):
    query_weight, key_weight, value_weight, output_weight, attention_gain, router_weight, mixture_gain, gate_weight, up_weight, down_weight = params
    highest = lax.Precision.HIGHEST
    segment, position, valid_slot = seq_layout(length_block)
    slot_index = jnp.arange(TOK_DEV, dtype=jnp.int32)
    valid_rows = valid_slot.astype(token_block.dtype)[:, None]
    normed_first = low(token_block * rms_scale(token_block) * attention_gain)
    query_raw = low_back(matmul(normed_first, query_weight)).reshape(TOK_DEV, HEADS, HEAD_DIM)
    key_raw = low_back(matmul(normed_first, key_weight)).reshape(TOK_DEV, KV_HEADS, HEAD_DIM)
    value_rows = low(low_back(matmul(normed_first, value_weight))).reshape(TOK_DEV, KV_HEADS, HEAD_DIM)
    cosine, sine_part = rope_tables(position)
    query_rot = low(rotate(query_raw, cosine, sine_part))
    key_rot = low(rotate(key_raw, cosine, sine_part))
    group_size = HEADS // KV_HEADS
    key_heads = jnp.repeat(key_rot, group_size, axis=1)
    value_heads = jnp.repeat(value_rows, group_size, axis=1)
    scores = low_back(jnp.einsum('thd,shd->hts', query_rot, key_heads, precision=highest) * (1.0 / math.sqrt(HEAD_DIM)))
    allowed = (segment[:, None] == segment[None, :]) & (slot_index[None, :] <= slot_index[:, None])
    probability = jax.nn.softmax(jnp.where(allowed[None], scores, -1e+30), axis=-1)
    mixed_heads = jnp.einsum('hts,shd->thd', low(probability), value_heads, precision=highest)
    attended = low(low_back(mixed_heads.reshape(TOK_DEV, HEADS * HEAD_DIM)))
    hidden = token_block + valid_rows * low_back(matmul(attended, output_weight))
    normed_second = low(hidden * rms_scale(hidden) * mixture_gain)
    logits = low_back(matmul(normed_second, router_weight))
    pick_mask = (index_block[:, :, None] == jnp.arange(EXPERTS, dtype=jnp.int32)[None, None, :]).astype(logits.dtype)
    picked = jnp.einsum('te,tke->tk', logits, pick_mask, precision=highest)
    gate_values = jax.nn.softmax(picked, axis=-1)
    combine = jnp.einsum('tk,tke->te', gate_values, pick_mask, precision=highest)
    gate_act = low_back(jnp.einsum('td,edf->tef', normed_second, gate_weight, precision=highest))
    up_act = low_back(jnp.einsum('td,edf->tef', normed_second, up_weight, precision=highest))
    inner_act = low(jax.nn.silu(gate_act) * up_act)
    expert_out = low_back(jnp.einsum('tef,efd->ted', inner_act, down_weight, precision=highest))
    mixture = jnp.einsum('te,ted->td', combine, expert_out, precision=highest)
    return hidden + valid_rows * mixture

def reference(tokens, sequence_lengths, expert_index, cotangent, query_weight, key_weight, value_weight, output_weight, attention_gain, router_weight, mixture_gain, gate_weight, up_weight, down_weight):
    params = (query_weight.astype(jnp.float32), key_weight.astype(jnp.float32), value_weight.astype(jnp.float32), output_weight.astype(jnp.float32), attention_gain.astype(jnp.float32), router_weight.astype(jnp.float32), mixture_gain.astype(jnp.float32), gate_weight.astype(jnp.float32), up_weight.astype(jnp.float32), down_weight.astype(jnp.float32))
    index_blocks = expert_index.reshape(N_FSDP, TOK_DEV, TOP)

    def forward(token_values, param_values):
        token_blocks = token_values.reshape(N_FSDP, TOK_DEV, D)

        def run_block(block_items):
            return layer_block(param_values, block_items[0], block_items[1], block_items[2])
        outputs = lax.map(jax.checkpoint(run_block), (token_blocks, sequence_lengths, index_blocks))
        return outputs.reshape(N_FSDP * TOK_DEV, D)
    layer_out, pullback = jax.vjp(forward, tokens.astype(jnp.float32), params)
    grad_tokens, grad_params = pullback(cotangent.astype(jnp.float32))
    return (layer_out.astype(jnp.bfloat16), grad_tokens.astype(jnp.bfloat16), grad_params[0], grad_params[1], grad_params[2], grad_params[3], grad_params[4], grad_params[5], grad_params[6], grad_params[7], grad_params[8], grad_params[9])
```

```python
import math

import jax
import jax.numpy as jnp
from jax import lax
from jax.sharding import Mesh, PartitionSpec as P

D = 1024
HEADS = 16
KV_HEADS = 8
HEAD_DIM = 64
EXPERTS = 12
TOP = 8
SEQ_DEV = 4
TOK_DEV = 256
FF = 512
ALL = ("y", "x", "z", "core")


epsilon = 1e-06
rope_base = 10000.0


def shift(v, axis, s):
    n = lax.axis_size(axis)
    return lax.ppermute(v, axis, [(i, (i + s) % n) for i in range(n)])


def add_low(*terms):
    return sum(a.astype(jnp.float32) for a in terms).astype(jnp.bfloat16)


def group_gather(v):
    half = v.shape[0] // 2
    above = shift(v, "z", 1)
    below = shift(v, "z", -1)
    far = jnp.concatenate([shift(above[:half], "z", 1), shift(below[half:], "z", -1)], axis=0)
    blocks = []
    for block in (v, below, far, above):
        blocks += [block, shift(block, "core", 1)]
    return blocks


def ring_sum(parts, axis):
    half = parts[2].shape[0] // 2
    front = shift(parts[2][:half], axis, 1)
    back = shift(parts[2][half:], axis, -1)
    ahead = jnp.concatenate([add_low(parts[1][:half], front), parts[1][half:]], axis=0)
    behind = jnp.concatenate([parts[3][:half], add_low(parts[3][half:], back)], axis=0)
    return sum(a.astype(jnp.float32) for a in (parts[0], shift(ahead, axis, 1), shift(behind, axis, -1)))


def direct_sum(parts, axis):
    terms = (parts[0], shift(parts[1], axis, 1), shift(parts[2], axis, 2), shift(parts[3], axis, -1))
    return sum(a.astype(jnp.float32) for a in terms)


def group_sum(blocks):
    other = [shift(b, "core", 1) for b in blocks[1::2]]
    return ring_sum([add_low(a, b) for a, b in zip(blocks[::2], other)], "z")


def axis_sum(v, axis, dim, how):
    me = lax.axis_index(axis)
    parts = [lax.dynamic_index_in_dim(v, (me + k) % 4, dim, keepdims=False) for k in range(4)]
    return how(parts, axis)


def torus_sum(v, order, axes, how=ring_sum):
    axes = list(axes)
    for i, axis in enumerate(order):
        v = axis_sum(v, axis, axes.index(axis), how)
        axes.remove(axis)
        if i < len(order) - 1:
            v = v.astype(jnp.bfloat16)
    return v


def group_exchange(v):
    z, c = lax.axis_index("z"), lax.axis_index("core")
    keep = lax.dynamic_index_in_dim(v, c, 1, keepdims=False)
    got = shift(lax.dynamic_index_in_dim(v, 1 - c, 1, keepdims=False), "core", 1)
    first = jnp.where(c == 0, keep, got)
    second = jnp.where(c == 0, got, keep)
    both = jnp.stack([first, second], axis=1)
    parts = [lax.dynamic_index_in_dim(both, (z + k) % 4, 0, keepdims=False) for k in range(4)]
    came = [parts[0]] + [shift(parts[k], "z", k) for k in (1, 2, 3)]
    line = jnp.stack([came[0], came[3], came[2], came[1]] * 2, axis=0)
    return lax.dynamic_slice_in_dim(line, (4 - z) % 4, 4, axis=0)


def column_order():
    column = lax.broadcasted_iota(jnp.int32, (FF, FF), 1)
    feature = lax.broadcasted_iota(jnp.int32, (FF, FF), 0)
    return feature == (column // 4 % 16) * 32 + (column // 64) * 4 + column % 4


def expert_lanes():
    lane = lax.broadcasted_iota(jnp.int32, (EXPERTS, EXPERTS * 64), 1) // 64
    return lane == lax.broadcasted_iota(jnp.int32, (EXPERTS, EXPERTS * 64), 0)


def rms_scale(activations):
    return lax.rsqrt(jnp.mean(activations * activations, axis=1, keepdims=True) + epsilon)


def seq_layout(lengths):
    ends_at = jnp.cumsum(lengths)
    starts_at = ends_at - lengths
    slot_index = jnp.arange(TOK_DEV, dtype=jnp.int32)
    segment = jnp.sum((slot_index[:, None] >= ends_at[None, :]).astype(jnp.int32), axis=1)
    owners = segment[:, None] == jnp.arange(SEQ_DEV, dtype=jnp.int32)[None, :]
    begins = jnp.sum(jnp.where(owners, starts_at[None, :], 0), axis=1)
    return (segment, slot_index - begins, segment < SEQ_DEV)


def rope_tables(position):
    half_size = HEAD_DIM // 2
    frequency = rope_base ** (-2.0 * jnp.arange(half_size, dtype=jnp.float32) / HEAD_DIM)
    angles = position.astype(jnp.float32)[:, None] * frequency[None, :]
    return (jnp.cos(angles)[:, None, :], jnp.sin(angles)[:, None, :])


def rotate(operand, cosine, sine_part):
    half_size = operand.shape[-1] // 2
    first_half = operand[..., :half_size]
    second_half = operand[..., half_size:]
    return jnp.concatenate(
        [
            first_half * cosine - second_half * sine_part,
            second_half * cosine + first_half * sine_part,
        ],
        axis=-1,
    )


def norm_backward(activations, inv_rms, gain_values, grad_normed):
    grad_gain = jnp.sum(grad_normed * activations * inv_rms, axis=0)
    scaled_grad = grad_normed * gain_values
    grad_input = inv_rms * scaled_grad - activations * inv_rms**3 * jnp.mean(
        scaled_grad * activations, axis=1, keepdims=True
    )
    return (grad_input, grad_gain)


def shards(
    tokens,
    sequence_lengths,
    expert_index,
    cotangent,
    query_weight,
    key_weight,
    value_weight,
    output_weight,
    attention_gain,
    router_weight,
    mixture_gain,
    gate_weight,
    up_weight,
    down_weight,
):
    bfloat = jnp.bfloat16
    single = jnp.float32
    group_size = HEADS // KV_HEADS
    score_scale = 1.0 / math.sqrt(HEAD_DIM)
    wide = EXPERTS * 64
    small = jnp.concatenate(
        [router_weight, attention_gain[:, None], mixture_gain[:, None], jnp.zeros((8, 114), bfloat)], axis=1
    )
    attention_full = lax.all_gather(
        jnp.concatenate([query_weight, key_weight, value_weight, output_weight, small], axis=1),
        ALL, axis=0, tiled=True,
    )
    qkv_full = attention_full[:, :2048]
    output_full = attention_full[:, 2048:3072]
    router_full = attention_full[:, 3072:3084]
    gains = attention_full[:, 3084:3086].astype(single)
    attn_gain_full, mix_gain_full = gains[:, 0], gains[:, 1]
    order = column_order().astype(bfloat)
    gate_up = jnp.concatenate([gate_weight, up_weight], axis=0).reshape(24 * 8, FF)
    gate_up = jnp.dot(gate_up, order, preferred_element_type=single).astype(bfloat)
    gate_up = gate_up.reshape(24, 8, 8, 64).transpose(2, 1, 0, 3).reshape(4, 2, 8, 2 * wide)
    gate_up = group_exchange(gate_up).reshape(64, 2 * wide)
    gate_up_full = lax.all_gather(gate_up, ("y", "x"), axis=0, tiled=True)
    down_full = lax.all_gather(down_weight.reshape(48, D), ("y", "x"), axis=0, tiled=True)
    down_full = down_full.reshape(16, 12, 4, D).transpose(1, 0, 2, 3).reshape(wide, D)

    segment, position, valid_slot = seq_layout(sequence_lengths[0])
    slot_index = jnp.arange(TOK_DEV, dtype=jnp.int32)
    valid_rows = valid_slot.astype(single)[:, None]
    pick = jnp.any(
        expert_index[:, :, None] == jnp.arange(EXPERTS, dtype=jnp.int32)[None, None, :], axis=1
    ).astype(bfloat)
    grad_out = cotangent.astype(single)
    early = jnp.concatenate(
        [cotangent * valid_rows.astype(bfloat), pick, jnp.zeros((TOK_DEV, 116), bfloat)], axis=1
    )
    early = jnp.concatenate(group_gather(early), axis=0)
    grad_mixture = early[:, :D]
    pick_all = early[:, D : D + EXPERTS] > 0

    token_values = tokens.astype(single)
    inv_first = rms_scale(token_values)
    normed_first = (token_values * inv_first * attn_gain_full).astype(bfloat)
    qkv = jnp.dot(normed_first, qkv_full, preferred_element_type=single)
    query_raw, key_raw = qkv[:, :1024], qkv[:, 1024:1536]
    value_rows = qkv[:, 1536:].astype(bfloat).reshape(TOK_DEV, KV_HEADS, HEAD_DIM)
    cosine, sine_part = rope_tables(position)
    query_rot = (
        rotate(query_raw.reshape(TOK_DEV, HEADS, HEAD_DIM), cosine, sine_part)
        .astype(bfloat)
        .reshape(TOK_DEV, KV_HEADS, group_size, HEAD_DIM)
    )
    key_rot = rotate(key_raw.reshape(TOK_DEV, KV_HEADS, HEAD_DIM), cosine, sine_part).astype(bfloat)
    allowed = (segment[:, None] == segment[None, :]) & (slot_index[None, :] <= slot_index[:, None])

    raw_scores = jnp.einsum("tngd,snd->ngts", query_rot, key_rot, preferred_element_type=single)
    masked = jnp.where(allowed[None, None], raw_scores * score_scale, -1e30)
    row_max = jnp.max(masked, axis=-1, keepdims=True)
    exp_terms = jnp.exp(masked - row_max)
    probability = exp_terms / jnp.sum(exp_terms, axis=-1, keepdims=True)
    probability_low = probability.astype(bfloat)
    mixed_heads = jnp.einsum(
        "ngts,snd->tngd", probability_low, value_rows, preferred_element_type=single
    )
    attended = mixed_heads.reshape(TOK_DEV, HEADS * HEAD_DIM).astype(bfloat)
    branch = jnp.dot(attended, output_full, preferred_element_type=single)
    hidden = token_values + valid_rows * branch
    inv_second = rms_scale(hidden)
    normed_second = (hidden * inv_second * mix_gain_full).astype(bfloat)

    rows = jnp.concatenate(group_gather(normed_second), axis=0)
    logits = jnp.dot(rows, router_full, preferred_element_type=single)
    logits = jnp.where(pick_all, logits, -jnp.inf)
    terms = jnp.exp(logits - jnp.max(logits, axis=1, keepdims=True))
    combine = terms / jnp.sum(terms, axis=1, keepdims=True)
    lanes = expert_lanes().astype(bfloat)
    high = combine.astype(bfloat)
    low = (combine - high.astype(single)).astype(bfloat)
    combine_wide = jnp.dot(
        jnp.concatenate([high, low], axis=1), jnp.concatenate([lanes, lanes], axis=0),
        preferred_element_type=single,
    )
    acts = jnp.dot(rows, gate_up_full, preferred_element_type=single)
    gate_act, up_act = acts[:, :wide], acts[:, wide:]
    sigmoid_gate = jax.nn.sigmoid(gate_act)
    silu_gate = gate_act * sigmoid_gate
    inner_act = (silu_gate * up_act).astype(bfloat).astype(single)
    inner_scaled = (inner_act * combine_wide).astype(bfloat)
    mixture_part = jnp.dot(inner_scaled, down_full, preferred_element_type=single).astype(bfloat)
    grad_down = jnp.dot(grad_mixture, down_full.T, preferred_element_type=single)
    grad_gates = jnp.dot(
        inner_act * grad_down, lanes.T.astype(single), preferred_element_type=single,
        precision=lax.Precision.HIGH,
    )
    grad_logits = combine * (grad_gates - jnp.sum(combine * grad_gates, axis=1, keepdims=True))
    grad_logits = grad_logits.astype(bfloat)
    grad_inner = grad_down * combine_wide
    grad_acts = jnp.concatenate(
        [
            (grad_inner * up_act * sigmoid_gate * (1.0 + gate_act * (1.0 - sigmoid_gate))).astype(bfloat),
            (grad_inner * silu_gate).astype(bfloat),
        ],
        axis=1,
    )
    grad_rows = (
        jnp.dot(grad_acts, gate_up_full.T, preferred_element_type=single)
        + jnp.dot(grad_logits, router_full.T, preferred_element_type=single)
    ).astype(bfloat)
    blocks_of = lambda a: [a[i * TOK_DEV : (i + 1) * TOK_DEV] for i in range(8)]
    grad_normed_second = group_sum(blocks_of(grad_rows))
    mixture = group_sum(blocks_of(mixture_part))
    layer_out = (hidden + valid_rows * mixture).astype(bfloat)

    router_grad = jnp.dot(rows.T, grad_logits, preferred_element_type=single)
    gate_up_grad = jnp.dot(rows.T, grad_acts, preferred_element_type=single).astype(bfloat)
    down_grad = jnp.dot(inner_scaled.T, grad_mixture, preferred_element_type=single).astype(bfloat)
    gate_part = torus_sum(gate_up_grad[:, :wide].reshape(4, 4, 64, wide), "yx", "yx")
    up_part = torus_sum(gate_up_grad[:, wide:].reshape(4, 4, 64, wide), "xy", "yx")
    down_grad = down_grad.reshape(12, 16, 4, D).transpose(1, 0, 2, 3).reshape(4, 4, 48, D)
    down_owned = jnp.concatenate(
        [
            torus_sum(down_grad[..., : D // 2], "yx", "yx"),
            torus_sum(down_grad[..., D // 2 :], "xy", "yx"),
        ],
        axis=-1,
    ).reshape(12, 4, D)
    owned = jnp.stack([gate_part, up_part], axis=1).reshape(4, 2, 8, 2 * wide)
    owned = group_exchange(owned).reshape(8, 8, 24, 64).transpose(2, 1, 0, 3).reshape(24 * 8, FF)
    owned = jnp.dot(
        owned, order.T.astype(single), preferred_element_type=single, precision=lax.Precision.HIGHEST
    ).reshape(2, EXPERTS, 8, FF)
    gate_owned, up_owned = owned[0], owned[1]

    grad_hidden_norm, mixture_gain_grad = norm_backward(
        hidden, inv_second, mix_gain_full, grad_normed_second
    )
    grad_hidden = grad_out + grad_hidden_norm
    grad_branch = (valid_rows * grad_hidden).astype(bfloat)
    output_grad = jnp.dot(attended.T, grad_branch, preferred_element_type=single)
    grad_attended = (
        jnp.dot(grad_branch, output_full.T, preferred_element_type=single)
        .astype(bfloat)
        .reshape(TOK_DEV, KV_HEADS, group_size, HEAD_DIM)
    )
    grad_probability = jnp.einsum(
        "tngd,snd->ngts", grad_attended, value_rows, preferred_element_type=single
    )
    grad_values = (
        jnp.einsum("ngts,tngd->snd", probability_low, grad_attended, preferred_element_type=single)
        .astype(bfloat)
        .reshape(TOK_DEV, KV_HEADS * HEAD_DIM)
    )
    row_dot = jnp.sum(probability * grad_probability, axis=-1, keepdims=True)
    grad_scores = (probability * (grad_probability - row_dot)).astype(bfloat)
    grad_query_rot = (
        jnp.einsum("ngts,snd->tngd", grad_scores, key_rot, preferred_element_type=single)
        * score_scale
    )
    grad_key_rot = (
        jnp.einsum("ngts,tngd->snd", grad_scores, query_rot, preferred_element_type=single)
        * score_scale
    )
    grad_query = (
        rotate(grad_query_rot.reshape(TOK_DEV, HEADS, HEAD_DIM), cosine, -sine_part)
        .astype(bfloat)
        .reshape(TOK_DEV, HEADS * HEAD_DIM)
    )
    grad_key = (
        rotate(grad_key_rot, cosine, -sine_part)
        .astype(bfloat)
        .reshape(TOK_DEV, KV_HEADS * HEAD_DIM)
    )
    grad_qkv = jnp.concatenate([grad_query, grad_key, grad_values], axis=1)
    qkv_grad = jnp.dot(normed_first.T, grad_qkv, preferred_element_type=single)
    grad_normed_first = jnp.dot(grad_qkv, qkv_full.T, preferred_element_type=single)
    grad_tokens_norm, attention_gain_grad = norm_backward(
        token_values, inv_first, attn_gain_full, grad_normed_first
    )
    grad_tokens = (grad_hidden + grad_tokens_norm).astype(bfloat)

    small_grad = jnp.concatenate(
        [router_grad, attention_gain_grad[:, None], mixture_gain_grad[:, None], jnp.zeros((D, 114), single)],
        axis=1,
    )
    sums = []
    c = lax.axis_index("core")
    for part, turn in (
        (qkv_grad[:, :1024], "yxz"),
        (qkv_grad[:, 1024:], "xzy"),
        (jnp.concatenate([output_grad, small_grad], axis=1), "zyx"),
    ):
        part = part.reshape(4, 4, 4, 2, 8, -1)
        send = lax.dynamic_index_in_dim(part, 1 - c, 3, keepdims=False).astype(bfloat)
        keep = lax.dynamic_index_in_dim(part, c, 3, keepdims=False)
        both = (keep + shift(send, "core", 1).astype(single)).astype(bfloat)
        sums.append(torus_sum(both, turn, "yxz"))
    query_owned, key_value_owned, rest = sums
    return (
        layer_out,
        grad_tokens,
        query_owned,
        key_value_owned[:, :512],
        key_value_owned[:, 512:],
        rest[:, :1024],
        rest[:, 1036],
        rest[:, 1024:1036],
        rest[:, 1037],
        gate_owned,
        up_owned,
        down_owned,
    )


def solution(mesh):
    mesh = Mesh(mesh.devices.reshape(4, 4, 4, 2), ALL)
    rows, line, inner = P(ALL, None), P(ALL), P(None, ALL, None)
    return jax.shard_map(
        shards,
        mesh=mesh,
        in_specs=(rows,) * 8 + (line, rows, line) + (inner,) * 3,
        out_specs=(rows,) * 6 + (line, rows, line) + (inner,) * 3,
        check_vma=False,
    )
```

```python
import functools
import math

import jax
import jax.numpy as jnp
from jax import lax
from jax.experimental import pallas as pl
from jax.experimental.pallas import tpu as pltpu
from jax.sharding import Mesh, PartitionSpec as P

D = 1024
HEADS = 16
KV_HEADS = 8
HEAD_DIM = 64
EXPERTS = 12
TOP = 8
SEQ_DEV = 4
TOK_DEV = 256
FF = 512
WIDE = EXPERTS * 64
ALL = ("y", "x", "z", "core")


epsilon = 1e-06
rope_base = 10000.0
SCORE_SCALE = 1.0 / math.sqrt(HEAD_DIM)


def shift(v, axis, s):
    n = lax.axis_size(axis)
    return lax.ppermute(v, axis, [(i, (i + s) % n) for i in range(n)])


def add_low(*terms):
    return sum(a.astype(jnp.float32) for a in terms).astype(jnp.bfloat16)


def group_gather(v):
    half = v.shape[0] // 2
    above = shift(v, "z", 1)
    below = shift(v, "z", -1)
    far = jnp.concatenate([shift(above[:half], "z", 1), shift(below[half:], "z", -1)], axis=0)
    blocks = []
    for block in (v, below, far, above):
        blocks += [block, shift(block, "core", 1)]
    return blocks


def ring_sum(parts, axis):
    half = parts[2].shape[0] // 2
    front = shift(parts[2][:half], axis, 1)
    back = shift(parts[2][half:], axis, -1)
    ahead = jnp.concatenate([add_low(parts[1][:half], front), parts[1][half:]], axis=0)
    behind = jnp.concatenate([parts[3][:half], add_low(parts[3][half:], back)], axis=0)
    return sum(a.astype(jnp.float32) for a in (parts[0], shift(ahead, axis, 1), shift(behind, axis, -1)))


def direct_sum(parts, axis):
    terms = (parts[0], shift(parts[1], axis, 1), shift(parts[2], axis, 2), shift(parts[3], axis, -1))
    return sum(a.astype(jnp.float32) for a in terms)


def group_sum(blocks, how=ring_sum):
    other = [shift(b, "core", 1) for b in blocks[1::2]]
    return how([add_low(a, b) for a, b in zip(blocks[::2], other)], "z")


def axis_sum(v, axis, dim, how):
    me = lax.axis_index(axis)
    parts = [lax.dynamic_index_in_dim(v, (me + k) % 4, dim, keepdims=False) for k in range(4)]
    return how(parts, axis)


def torus_sum(v, order, axes, how=ring_sum):
    axes = list(axes)
    for i, axis in enumerate(order):
        v = axis_sum(v, axis, axes.index(axis), how)
        axes.remove(axis)
        if i < len(order) - 1:
            v = v.astype(jnp.bfloat16)
    return v


def axis_gather(v, axis):
    me = lax.axis_index(axis)
    parts = [v, shift(v, axis, -1), shift(v, axis, 2), shift(v, axis, 1)]
    line = jnp.stack(parts + parts[:3], axis=0)
    return lax.dynamic_slice_in_dim(line, (4 - me) % 4, 4, axis=0)


def down_packed(v):
    n = v.shape[0]
    rest = v[:, :, 768:].reshape(n, 3, 16, 256).swapaxes(1, 2).reshape(n, 16, 768)
    return jnp.concatenate([v[:, :, :768], rest], axis=1).reshape(n * 64, 768)


def down_unpacked(v):
    v = v.reshape(-1, 64, 768)
    rest = v[:, 48:].reshape(-1, 16, 3, 256).swapaxes(1, 2).reshape(-1, 48, 256)
    return jnp.concatenate([v[:, :48], rest], axis=2).reshape(-1, D)


def group_exchange(v):
    z, c = lax.axis_index("z"), lax.axis_index("core")
    keep = lax.dynamic_index_in_dim(v, c, 1, keepdims=False)
    got = shift(lax.dynamic_index_in_dim(v, 1 - c, 1, keepdims=False), "core", 1)
    first = jnp.where(c == 0, keep, got)
    second = jnp.where(c == 0, got, keep)
    both = jnp.stack([first, second], axis=1)
    parts = [lax.dynamic_index_in_dim(both, (z + k) % 4, 0, keepdims=False) for k in range(4)]
    came = [parts[0]] + [shift(parts[k], "z", k) for k in (1, 2, 3)]
    line = jnp.stack([came[0], came[3], came[2], came[1]] * 2, axis=0)
    return lax.dynamic_slice_in_dim(line, (4 - z) % 4, 4, axis=0)


def column_order():
    column = lax.broadcasted_iota(jnp.int32, (FF, FF), 1)
    feature = lax.broadcasted_iota(jnp.int32, (FF, FF), 0)
    return feature == (column // 4 % 16) * 32 + (column // 64) * 4 + column % 4


def spread_order():
    column = lax.broadcasted_iota(jnp.int32, (WIDE, WIDE), 1)
    feature = lax.broadcasted_iota(jnp.int32, (WIDE, WIDE), 0)
    return feature == (column % 48) // 4 * 64 + column // 48 * 4 + column % 4


def expert_lanes():
    expert = (lax.broadcasted_iota(jnp.int32, (128, WIDE), 1) % 48) // 4
    return expert == lax.broadcasted_iota(jnp.int32, (128, WIDE), 0)


def seq_layout(lengths):
    ends_at = jnp.cumsum(lengths)
    starts_at = ends_at - lengths
    slot_index = jnp.arange(TOK_DEV, dtype=jnp.int32)
    segment = jnp.sum((slot_index[:, None] >= ends_at[None, :]).astype(jnp.int32), axis=1)
    owners = segment[:, None] == jnp.arange(SEQ_DEV, dtype=jnp.int32)[None, :]
    begins = jnp.sum(jnp.where(owners, starts_at[None, :], 0), axis=1)
    return (segment, slot_index - begins, segment < SEQ_DEV)


def rope_tables(position):
    half_size = HEAD_DIM // 2
    frequency = rope_base ** (-2.0 * jnp.arange(half_size, dtype=jnp.float32) / HEAD_DIM)
    angles = position.astype(jnp.float32)[:, None] * frequency[None, :]
    cosine, sine_part = jnp.cos(angles), jnp.sin(angles)
    return (
        jnp.concatenate([cosine] * 4, axis=1),
        jnp.concatenate([-sine_part, sine_part] * 2, axis=1),
    )


def across(a, b):
    return lax.dot_general(a, b, (((1,), (1,)), ((), ())), preferred_element_type=jnp.float32)


def down_rows(a, b):
    return lax.dot_general(a, b, (((0,), (0,)), ((), ())), preferred_element_type=jnp.float32)


def straight(a, b):
    return jnp.dot(a, b, preferred_element_type=jnp.float32)


def turn(x, cosine, sine_part):
    lane = lax.broadcasted_iota(jnp.int32, x.shape, 1) % HEAD_DIM
    other = jnp.where(lane < HEAD_DIM // 2, pltpu.roll(x, 96, 1), pltpu.roll(x, 32, 1))
    return x * cosine + other * sine_part


def cut(k, size):
    return pl.ds(pl.multiple_of(k * size, size), size)


def kernel_call(body, outs, scratch=(), flops=0, moved=0, **more):
    return pl.pallas_call(
        body,
        out_shape=[jax.ShapeDtypeStruct(shape, kind) for shape, kind in outs],
        scratch_shapes=list(scratch),
        compiler_params=pltpu.CompilerParams(vmem_limit_bytes=60 * 1024 * 1024),
        cost_estimate=pl.CostEstimate(flops=flops, bytes_accessed=moved, transcendentals=0),
        **more,
    )


def mask_bias(seg_col, seg_row):
    row = lax.broadcasted_iota(jnp.int32, (TOK_DEV, TOK_DEV), 0)
    column = lax.broadcasted_iota(jnp.int32, (TOK_DEV, TOK_DEV), 1)
    return jnp.where((seg_col == seg_row) & (column <= row), 0.0, -1e30)


def attend_body(tok, gain, cosine, sine_part, seg_col, seg_row, wq, wkv, normed, turned, value, out, lse):
    x = tok[...].astype(jnp.float32)
    scale = lax.rsqrt(jnp.mean(x * x, axis=1, keepdims=True) + epsilon)
    normed[...] = (x * scale * gain[...]).astype(jnp.bfloat16)
    cos, sin = cosine[...], sine_part[...]

    def turned_pair(raw):
        both = [turn(raw[:, :128], cos, sin), turn(raw[:, 128:], cos, sin)]
        return jnp.concatenate(both, axis=1).astype(jnp.bfloat16)

    @pl.loop(0, 4)
    def _(k):
        turned[:, cut(k, 256)] = turned_pair(straight(normed[...], wq[:, cut(k, 256)]))

    @pl.loop(0, 2)
    def _(k):
        turned[:, cut(k + 4, 256)] = turned_pair(straight(normed[...], wkv[:, cut(k, 256)]))
        value[:, cut(k, 256)] = straight(normed[...], wkv[:, cut(k + 2, 256)]).astype(jnp.bfloat16)

    bias = mask_bias(seg_col[...], seg_row[...])
    lse[...] = jnp.zeros_like(lse)
    lane = lax.broadcasted_iota(jnp.int32, (TOK_DEV, 128), 1)

    @pl.loop(0, 4)
    def _(p):
        queries = turned[:, cut(p, 256)]
        keys = turned[:, pl.ds(pl.multiple_of(1024 + p * 128, 128), 128)]
        values = value[:, cut(p, 128)]
        done, logs = [], lse[...]
        for h in range(4):
            side = slice(h // 2 * 64, h // 2 * 64 + 64)
            s = across(queries[:, h * 64 : h * 64 + 64], keys[:, side]) * SCORE_SCALE + bias
            top = jnp.max(s, axis=1, keepdims=True)
            e = jnp.exp(s - top)
            total = jnp.sum(e, axis=1, keepdims=True)
            prob = (e / total).astype(jnp.bfloat16)
            done.append(straight(prob, values[:, side]))
            logs = jnp.where(lane == p * 4 + h, top + jnp.log(total), logs)
        lse[...] = logs
        out[:, cut(p, 256)] = jnp.concatenate(done, axis=1).astype(jnp.bfloat16)


def hidden_body(tok, valid, attended, weight, gain, hidden, normed):
    keep = valid[...]

    @pl.loop(0, 4)
    def _(k):
        branch = straight(attended[...], weight[:, cut(k, 256)])
        hidden[:, cut(k, 256)] = tok[:, cut(k, 256)].astype(jnp.float32) + keep * branch

    x = hidden[...]
    scale = lax.rsqrt(jnp.mean(x * x, axis=1, keepdims=True) + epsilon)
    normed[...] = (x * scale * gain[...]).astype(jnp.bfloat16)


def expert_body(
    x0, x1, early0, early1, router, gate_up, down, lanes,
    mixed, grad_x, inner_out, acts_out, logit_out, x, grads,
):
    for i, (block, early) in enumerate(((x0, early0), (x1, early1))):
        x[i * TOK_DEV : (i + 1) * TOK_DEV, :] = block[...]
        grads[i * TOK_DEV : (i + 1) * TOK_DEV, :] = early[...]
    logits = straight(x[...], router[...])
    routed = grads[:, D:].astype(jnp.float32) > 0.5
    logits = jnp.where(routed, logits, -1e30)
    terms = jnp.where(routed, jnp.exp(logits - jnp.max(logits, axis=1, keepdims=True)), 0.0)
    combine = terms / jnp.sum(terms, axis=1, keepdims=True)
    high = combine.astype(jnp.bfloat16)
    low = (combine - high.astype(jnp.float32)).astype(jnp.bfloat16)
    grad_gates = jnp.zeros(combine.shape, jnp.float32)
    for t in range(3):
        cols, cols_up = slice(t * 256, t * 256 + 256), slice(WIDE + t * 256, WIDE + t * 256 + 256)
        gate = straight(x[...], gate_up[:, cols])
        up = straight(x[...], gate_up[:, cols_up])
        spread = straight(high, lanes[:, cols]) + straight(low, lanes[:, cols])
        grad_down = across(grads[:, :D], down[cols, :])
        sig = 1.0 / (1.0 + jnp.exp(-gate))
        silu = gate * sig
        inner = (silu * up).astype(jnp.bfloat16).astype(jnp.float32)
        inner_out[:, cols] = (inner * spread).astype(jnp.bfloat16)
        grad_inner = grad_down * spread
        acts_out[:, cols] = (grad_inner * up * sig * (1.0 + gate * (1.0 - sig))).astype(jnp.bfloat16)
        acts_out[:, cols_up] = (grad_inner * silu).astype(jnp.bfloat16)
        product = inner * grad_down
        product_high = product.astype(jnp.bfloat16)
        product_low = (product - product_high.astype(jnp.float32)).astype(jnp.bfloat16)
        grad_gates += across(product_high, lanes[:, cols]) + across(product_low, lanes[:, cols])
    grad_logits = combine * (grad_gates - jnp.sum(combine * grad_gates, axis=1, keepdims=True))
    logit_out[...] = grad_logits.astype(jnp.bfloat16)

    @pl.loop(0, 4)
    def _(k):
        back = across(acts_out[...], gate_up[cut(k, 256), :])
        back += across(logit_out[...], router[cut(k, 256), :])
        grad_x[:, cut(k, 256)] = back.astype(jnp.bfloat16)
        mixed[:, cut(k, 256)] = straight(inner_out[...], down[:, cut(k, 256)]).astype(jnp.bfloat16)


def hidden_grad_body(dy, hidden, cot, gain, valid, weight, grad_hidden, branch, grad_att, gain_grad):
    x, d = hidden[...], dy[...]
    scale = lax.rsqrt(jnp.mean(x * x, axis=1, keepdims=True) + epsilon)
    gain_grad[...] = jnp.sum(d * x * scale, axis=0, keepdims=True)
    g = d * gain[...]
    dx = scale * g - x * scale * scale * scale * jnp.mean(g * x, axis=1, keepdims=True)
    total = cot[...].astype(jnp.float32) + dx
    grad_hidden[...] = total
    branch[...] = (valid[...] * total).astype(jnp.bfloat16)

    @pl.loop(0, 4)
    def _(k):
        grad_att[:, cut(k, 256)] = across(branch[...], weight[cut(k, 256), :]).astype(jnp.bfloat16)


def attend_grad_body(
    tok, gain, cosine, sine_part, seg_col, seg_row, wq, wkv, turned, value, lse, grad_att, grad_hidden,
    grad_qkv, grad_tok, gain_grad, grad_normed,
):
    bias = mask_bias(seg_col[...], seg_row[...])
    cos, sin = cosine[...], -sine_part[...]
    lane = lax.broadcasted_iota(jnp.int32, (TOK_DEV, 128), 1)

    @pl.loop(0, 4)
    def _(p):
        queries = turned[:, cut(p, 256)]
        keys = turned[:, pl.ds(pl.multiple_of(1024 + p * 128, 128), 128)]
        values = value[:, cut(p, 128)]
        grads = grad_att[:, cut(p, 256)]
        for_query, for_key, for_value = [], [0.0, 0.0], [0.0, 0.0]
        for h in range(4):
            side = slice(h // 2 * 64, h // 2 * 64 + 64)
            own = slice(h * 64, h * 64 + 64)
            log_total = jnp.sum(jnp.where(lane == p * 4 + h, lse[...], 0.0), axis=1, keepdims=True)
            prob = jnp.exp(across(queries[:, own], keys[:, side]) * SCORE_SCALE + bias - log_total)
            grad_prob = across(grads[:, own], values[:, side])
            for_value[h // 2] += down_rows(prob.astype(jnp.bfloat16), grads[:, own])
            row_dot = jnp.sum(prob * grad_prob, axis=1, keepdims=True)
            grad_scores = (prob * (grad_prob - row_dot)).astype(jnp.bfloat16)
            for_query.append(straight(grad_scores, keys[:, side]) * SCORE_SCALE)
            for_key[h // 2] += down_rows(grad_scores, queries[:, own]) * SCORE_SCALE
        q = jnp.concatenate(for_query, axis=1)
        q = jnp.concatenate([turn(q[:, :128], cos, sin), turn(q[:, 128:], cos, sin)], axis=1)
        grad_qkv[:, cut(p, 256)] = q.astype(jnp.bfloat16)
        k = turn(jnp.concatenate(for_key, axis=1), cos, sin)
        grad_qkv[:, pl.ds(pl.multiple_of(1024 + p * 128, 128), 128)] = k.astype(jnp.bfloat16)
        v = jnp.concatenate(for_value, axis=1)
        grad_qkv[:, pl.ds(pl.multiple_of(1536 + p * 128, 128), 128)] = v.astype(jnp.bfloat16)

    @pl.loop(0, 4)
    def _(k):
        back = across(grad_qkv[:, :D], wq[cut(k, 256), :])
        grad_normed[:, cut(k, 256)] = back + across(grad_qkv[:, D:], wkv[cut(k, 256), :])

    x, d = tok[...].astype(jnp.float32), grad_normed[...]
    scale = lax.rsqrt(jnp.mean(x * x, axis=1, keepdims=True) + epsilon)
    gain_grad[...] = jnp.sum(d * x * scale, axis=0, keepdims=True)
    g = d * gain[...]
    dx = scale * g - x * scale * scale * scale * jnp.mean(g * x, axis=1, keepdims=True)
    grad_tok[...] = (grad_hidden[...] + dx).astype(jnp.bfloat16)


def shards(
    tokens,
    sequence_lengths,
    expert_index,
    cotangent,
    query_weight,
    key_weight,
    value_weight,
    output_weight,
    attention_gain,
    router_weight,
    mixture_gain,
    gate_weight,
    up_weight,
    down_weight,
):
    bfloat = jnp.bfloat16
    single = jnp.float32
    c = lax.axis_index("core")
    small = jnp.concatenate(
        [router_weight, jnp.zeros((8, 114), bfloat), attention_gain[:, None], mixture_gain[:, None]], axis=1
    )
    left = jnp.concatenate([query_weight, output_weight[:, : D // 2], small], axis=1)
    right = jnp.concatenate([key_weight, value_weight, output_weight[:, D // 2 :], small], axis=1)
    got = shift(jnp.where(c == 0, right, left), "core", 1)
    mine = jnp.where(c == 0, left, right)
    mine = jnp.where(c == 0, jnp.concatenate([mine, got]), jnp.concatenate([got, mine]))
    mine = axis_gather(mine, "z").reshape(64, 1664)
    segment, position, valid_slot = seq_layout(sequence_lengths[0])
    seg_col, seg_row = segment[:, None], segment[None, :]
    valid_rows = valid_slot.astype(single)[:, None]
    cosine, sine_part = rope_tables(position)
    pick = jnp.any(
        expert_index[:, :, None] == jnp.arange(128, dtype=jnp.int32)[None, None, :], axis=1
    ).astype(bfloat)
    early = jnp.concatenate([cotangent * valid_rows.astype(bfloat), pick], axis=1)
    early, mine = lax.optimization_barrier((early, mine))
    early = group_gather(early)
    first = axis_gather(mine[:, :D], "x").reshape(256, D)
    second = axis_gather(mine[:, D:], "y").reshape(256, 640)
    first = axis_gather(first, "y").reshape(D, D)
    second = axis_gather(second, "x").reshape(4, 4, 64, 640).swapaxes(0, 1).reshape(D, 640)
    first_got, second_got = shift(first, "core", 1), shift(second, "core", 1)
    query_full = jnp.where(c == 0, first, first_got)
    key_value_full = jnp.where(c == 0, first_got, first)
    router_full = second[:, 512:]
    output_full = jnp.where(
        c == 0,
        jnp.concatenate([second[:, :512], second_got[:, :512]], axis=1),
        jnp.concatenate([second_got[:, :512], second[:, :512]], axis=1),
    )
    gains = router_full[:, 126:].astype(single).T
    attn_gain_full, mix_gain_full = gains[:1], gains[1:]
    order = column_order().astype(bfloat)
    spread = spread_order().astype(bfloat)
    gate_up = jnp.concatenate([gate_weight, up_weight], axis=0).reshape(24 * 8, FF)
    gate_up = jnp.dot(gate_up, order, preferred_element_type=single).astype(bfloat)
    gate_up = gate_up.reshape(24, 8, 8, 64).transpose(2, 1, 0, 3).reshape(4, 2, 8, 2 * WIDE)
    gate_up = group_exchange(gate_up).reshape(128, WIDE)
    gate_up = jnp.dot(gate_up, spread, preferred_element_type=single).astype(bfloat).reshape(64, 2 * WIDE)
    share = jnp.concatenate([gate_up, down_packed(down_weight.reshape(1, 48, D))], axis=1)
    share = lax.all_gather(share, ("y", "x"), axis=0, tiled=True)
    gate_up_full, down_full = share[:, : 2 * WIDE], down_unpacked(share[:, 2 * WIDE :])
    lanes = expert_lanes().astype(bfloat)

    normed_first, turned, value_rows, attended, lse = kernel_call(
        attend_body,
        [((256, D), bfloat), ((256, 1536), bfloat), ((256, 512), bfloat), ((256, D), bfloat), ((256, 128), single)],
        flops=2 * 10**9, moved=8 * 10**6,
    )(tokens, attn_gain_full, cosine, sine_part, seg_col, seg_row, query_full, key_value_full)
    hidden, normed_second = kernel_call(
        hidden_body, [((256, D), single), ((256, D), bfloat)], flops=10**9, moved=4 * 10**6
    )(tokens, valid_rows, attended, output_full, mix_gain_full)

    blocks = group_gather(normed_second)
    mixed, grad_rows, inner_scaled, grad_acts, grad_logits = [], [], [], [], []
    for i in (0, 2, 6, 4):
        results = kernel_call(
            expert_body,
            [((512, D), bfloat), ((512, D), bfloat), ((512, WIDE), bfloat), ((512, 2 * WIDE), bfloat), ((512, 128), bfloat)],
            scratch=[pltpu.VMEM((512, D), bfloat), pltpu.VMEM((512, D + 128), bfloat)],
            flops=6 * 10**9, moved=12 * 10**6,
        )(blocks[i], blocks[i + 1], early[i], early[i + 1], router_full, gate_up_full, down_full, lanes)
        for kept, result in zip((mixed, grad_rows, inner_scaled, grad_acts, grad_logits), results):
            kept.append(result)
    place = [0, 1, 3, 2]
    halves = lambda a: [a[place[k]][j * TOK_DEV : (j + 1) * TOK_DEV] for k in range(4) for j in range(2)]
    grad_normed_second = group_sum(halves(grad_rows), direct_sum)
    mixed, grad_normed_second = lax.optimization_barrier((mixed, grad_normed_second))
    rows = jnp.concatenate([blocks[i + j] for i in (0, 2, 6, 4) for j in (0, 1)], axis=0)
    grad_mixture = jnp.concatenate([early[i + j][:, :D] for i in (0, 2, 6, 4) for j in (0, 1)], axis=0)
    whole = lambda a: jnp.concatenate(a, axis=0)
    inner_scaled, grad_acts, grad_logits = whole(inner_scaled), whole(grad_acts), whole(grad_logits)

    grad_hidden, grad_branch, grad_attended, mixture_gain_grad = kernel_call(
        hidden_grad_body,
        [((256, D), single), ((256, D), bfloat), ((256, D), bfloat), ((1, D), single)],
        flops=10**9, moved=6 * 10**6,
    )(grad_normed_second, hidden, cotangent, mix_gain_full, valid_rows, output_full)
    grad_qkv, grad_tokens, attention_gain_grad = kernel_call(
        attend_grad_body,
        [((256, 2048), bfloat), ((256, D), bfloat), ((1, D), single)],
        scratch=[pltpu.VMEM((256, D), single)],
        flops=3 * 10**9, moved=12 * 10**6,
    )(
        tokens, attn_gain_full, cosine, sine_part, seg_col, seg_row, query_full, key_value_full, turned, value_rows, lse,
        grad_attended, grad_hidden,
    )

    gate_up_grad = down_rows(rows, grad_acts).astype(bfloat)
    down_grad = down_rows(inner_scaled, grad_mixture).astype(bfloat).reshape(16, 48, D)
    router_grad = down_rows(rows, grad_logits)
    share = jnp.concatenate([gate_up_grad, down_packed(down_grad)], axis=1)
    share = lax.psum_scatter(share, ("y", "x"), scatter_dimension=0, tiled=True).astype(single)
    down_owned = down_unpacked(share[:, 2 * WIDE :]).reshape(12, 4, D)
    owned = share[:, : 2 * WIDE].reshape(128, WIDE)
    exact = lax.Precision.HIGHEST
    owned = jnp.dot(owned, spread.T.astype(single), preferred_element_type=single, precision=exact)
    owned = group_exchange(owned.reshape(4, 2, 8, 2 * WIDE)).reshape(8, 8, 24, 64).transpose(2, 1, 0, 3).reshape(24 * 8, FF)
    owned = jnp.dot(owned, order.T.astype(single), preferred_element_type=single, precision=exact)
    owned = owned.reshape(2, EXPERTS, 8, FF)
    gate_owned, up_owned = owned[0], owned[1]

    mixture = group_sum(halves(mixed))
    layer_out = (hidden + valid_rows * mixture).astype(bfloat)

    output_grad = down_rows(attended, grad_branch)
    qkv_grad = down_rows(normed_first, grad_qkv)
    small_grad = jnp.concatenate(
        [router_grad[:, :126], attention_gain_grad.T, mixture_gain_grad.T], axis=1
    )
    sums = []
    for part, turn_order in (
        (output_grad, "xzy"),
        (qkv_grad[:, :1024], "yxz"),
        (jnp.concatenate([qkv_grad[:, 1024:], small_grad], axis=1), "zyx"),
    ):
        part = part.reshape(4, 4, 4, 2, 8, -1)
        send = lax.dynamic_index_in_dim(part, 1 - c, 3, keepdims=False).astype(bfloat)
        keep = lax.dynamic_index_in_dim(part, c, 3, keepdims=False)
        both = (keep + shift(send, "core", 1).astype(single)).astype(bfloat)
        sums.append(torus_sum(both, turn_order, "yxz", direct_sum))
    output_owned, query_owned, rest = sums
    return (
        layer_out,
        grad_tokens,
        query_owned,
        rest[:, :512],
        rest[:, 512:1024],
        output_owned,
        rest[:, 1150],
        rest[:, 1024:1036],
        rest[:, 1151],
        gate_owned,
        up_owned,
        down_owned,
    )


def solution(mesh):
    mesh = Mesh(mesh.devices.reshape(4, 4, 4, 2), ALL)
    rows, line, inner = P(ALL, None), P(ALL), P(None, ALL, None)
    return jax.shard_map(
        shards,
        mesh=mesh,
        in_specs=(rows,) * 8 + (line, rows, line) + (inner,) * 3,
        out_specs=(rows,) * 6 + (line, rows, line) + (inner,) * 3,
        check_vma=False,
    )
```

```python
import functools
import math

import jax
import jax.numpy as jnp
from jax import lax
from jax.experimental import pallas as pl
from jax.experimental.pallas import tpu as pltpu
from jax.sharding import Mesh, PartitionSpec as P

D = 1024
HEADS = 16
KV_HEADS = 8
HEAD_DIM = 64
EXPERTS = 12
TOP = 8
SEQ_DEV = 4
TOK_DEV = 256
FF = 512
WIDE = EXPERTS * 64
ALL = ("y", "x", "z", "core")


epsilon = 1e-06
rope_base = 10000.0
SCORE_SCALE = 1.0 / math.sqrt(HEAD_DIM)


def shift(v, axis, s):
    n = lax.axis_size(axis)
    return lax.ppermute(v, axis, [(i, (i + s) % n) for i in range(n)])


def add_low(*terms):
    return sum(a.astype(jnp.float32) for a in terms).astype(jnp.bfloat16)


def group_gather(v):
    half = v.shape[0] // 2
    above = shift(v, "z", 1)
    below = shift(v, "z", -1)
    far = jnp.concatenate([shift(above[:half], "z", 1), shift(below[half:], "z", -1)], axis=0)
    blocks = []
    for block in (v, below, far, above):
        blocks += [block, shift(block, "core", 1)]
    return blocks


def ring_sum(parts, axis):
    half = parts[2].shape[0] // 2
    front = shift(parts[2][:half], axis, 1)
    back = shift(parts[2][half:], axis, -1)
    ahead = jnp.concatenate([add_low(parts[1][:half], front), parts[1][half:]], axis=0)
    behind = jnp.concatenate([parts[3][:half], add_low(parts[3][half:], back)], axis=0)
    return sum(a.astype(jnp.float32) for a in (parts[0], shift(ahead, axis, 1), shift(behind, axis, -1)))


def direct_sum(parts, axis):
    terms = (parts[0], shift(parts[1], axis, 1), shift(parts[2], axis, 2), shift(parts[3], axis, -1))
    return sum(a.astype(jnp.float32) for a in terms)


def group_sum(blocks, how=ring_sum):
    other = [shift(b, "core", 1) for b in blocks[1::2]]
    return how([add_low(a, b) for a, b in zip(blocks[::2], other)], "z")


def axis_sum(v, axis, dim, how):
    me = lax.axis_index(axis)
    parts = [lax.dynamic_index_in_dim(v, (me + k) % 4, dim, keepdims=False) for k in range(4)]
    return how(parts, axis)


def torus_sum(v, order, axes, how=ring_sum):
    axes = list(axes)
    for i, axis in enumerate(order):
        v = axis_sum(v, axis, axes.index(axis), how)
        axes.remove(axis)
        if i < len(order) - 1:
            v = v.astype(jnp.bfloat16)
    return v


def axis_gather(v, axis):
    me = lax.axis_index(axis)
    parts = [v, shift(v, axis, -1), shift(v, axis, 2), shift(v, axis, 1)]
    line = jnp.stack(parts + parts[:3], axis=0)
    return lax.dynamic_slice_in_dim(line, (4 - me) % 4, 4, axis=0)


def down_packed(v):
    n = v.shape[0]
    rest = v[:, :, 768:].reshape(n, 3, 16, 256).swapaxes(1, 2).reshape(n, 16, 768)
    return jnp.concatenate([v[:, :, :768], rest], axis=1).reshape(n * 64, 768)


def down_unpacked(v):
    v = v.reshape(-1, 64, 768)
    rest = v[:, 48:].reshape(-1, 16, 3, 256).swapaxes(1, 2).reshape(-1, 48, 256)
    return jnp.concatenate([v[:, :48], rest], axis=2).reshape(-1, D)


def group_exchange(v):
    z, c = lax.axis_index("z"), lax.axis_index("core")
    keep = lax.dynamic_index_in_dim(v, c, 1, keepdims=False)
    got = shift(lax.dynamic_index_in_dim(v, 1 - c, 1, keepdims=False), "core", 1)
    first = jnp.where(c == 0, keep, got)
    second = jnp.where(c == 0, got, keep)
    both = jnp.stack([first, second], axis=1)
    parts = [lax.dynamic_index_in_dim(both, (z + k) % 4, 0, keepdims=False) for k in range(4)]
    came = [parts[0]] + [shift(parts[k], "z", k) for k in (1, 2, 3)]
    line = jnp.stack([came[0], came[3], came[2], came[1]] * 2, axis=0)
    return lax.dynamic_slice_in_dim(line, (4 - z) % 4, 4, axis=0)


def column_order():
    column = lax.broadcasted_iota(jnp.int32, (FF, FF), 1)
    feature = lax.broadcasted_iota(jnp.int32, (FF, FF), 0)
    return feature == (column // 4 % 16) * 32 + (column // 64) * 4 + column % 4


def spread_order():
    column = lax.broadcasted_iota(jnp.int32, (WIDE, WIDE), 1)
    feature = lax.broadcasted_iota(jnp.int32, (WIDE, WIDE), 0)
    return feature == (column % 48) // 4 * 64 + column // 48 * 4 + column % 4


def expert_lanes():
    expert = (lax.broadcasted_iota(jnp.int32, (128, WIDE), 1) % 48) // 4
    return expert == lax.broadcasted_iota(jnp.int32, (128, WIDE), 0)


def seq_layout(lengths):
    ends_at = jnp.cumsum(lengths)
    starts_at = ends_at - lengths
    slot_index = jnp.arange(TOK_DEV, dtype=jnp.int32)
    segment = jnp.sum((slot_index[:, None] >= ends_at[None, :]).astype(jnp.int32), axis=1)
    owners = segment[:, None] == jnp.arange(SEQ_DEV, dtype=jnp.int32)[None, :]
    begins = jnp.sum(jnp.where(owners, starts_at[None, :], 0), axis=1)
    return (segment, slot_index - begins, segment < SEQ_DEV)


def rope_tables(position):
    half_size = HEAD_DIM // 2
    frequency = rope_base ** (-2.0 * jnp.arange(half_size, dtype=jnp.float32) / HEAD_DIM)
    angles = position.astype(jnp.float32)[:, None] * frequency[None, :]
    cosine, sine_part = jnp.cos(angles), jnp.sin(angles)
    return (
        jnp.concatenate([cosine] * 4, axis=1),
        jnp.concatenate([-sine_part, sine_part] * 2, axis=1),
    )


def across(a, b):
    return lax.dot_general(a, b, (((1,), (1,)), ((), ())), preferred_element_type=jnp.float32)


def down_rows(a, b):
    return lax.dot_general(a, b, (((0,), (0,)), ((), ())), preferred_element_type=jnp.float32)


def straight(a, b):
    return jnp.dot(a, b, preferred_element_type=jnp.float32)


def turn(x, cosine, sine_part):
    lane = lax.broadcasted_iota(jnp.int32, x.shape, 1) % HEAD_DIM
    other = jnp.where(lane < HEAD_DIM // 2, pltpu.roll(x, 96, 1), pltpu.roll(x, 32, 1))
    return x * cosine + other * sine_part


def cut(k, size):
    return pl.ds(pl.multiple_of(k * size, size), size)


ALL_OF = pl.BlockSpec(memory_space=pltpu.VMEM)
QKV_PART = pl.BlockSpec((D, 2 * D), lambda i: (0, 0))
OUT_PART = pl.BlockSpec((D, D), lambda i: (0, 2))
ROUTER_PART = pl.BlockSpec((D, 128), lambda i: (0, 24))
GATE_UP_PART = pl.BlockSpec((D, 2 * WIDE), lambda i: (0, 0))


def kernel_call(body, outs, scratch=(), flops=0, moved=0, **more):
    return pl.pallas_call(
        body,
        out_shape=[jax.ShapeDtypeStruct(shape, kind) for shape, kind in outs],
        grid=(1,),
        scratch_shapes=list(scratch),
        compiler_params=pltpu.CompilerParams(vmem_limit_bytes=60 * 1024 * 1024),
        cost_estimate=pl.CostEstimate(flops=flops, bytes_accessed=moved, transcendentals=0),
        **more,
    )


def mask_bias(seg_col, seg_row):
    row = lax.broadcasted_iota(jnp.int32, (TOK_DEV, TOK_DEV), 0)
    column = lax.broadcasted_iota(jnp.int32, (TOK_DEV, TOK_DEV), 1)
    return jnp.where((seg_col == seg_row) & (column <= row), 0.0, -1e30)


def attend_body(
    tok, gain, second_gain, cosine, sine_part, seg_col, seg_row, valid, lanes, weight, weight_out,
    normed, turned, value, out, lse, hidden, normed_second,
):
    x = tok[...].astype(jnp.float32)
    scale = lax.rsqrt(jnp.mean(x * x, axis=1, keepdims=True) + epsilon)
    normed[...] = (x * scale * gain[...]).astype(jnp.bfloat16)
    cos, sin = cosine[...], sine_part[...]

    def turned_pair(raw):
        both = [turn(raw[:, :128], cos, sin), turn(raw[:, 128:], cos, sin)]
        return jnp.concatenate(both, axis=1).astype(jnp.bfloat16)

    @pl.loop(0, 6)
    def _(k):
        turned[:, cut(k, 256)] = turned_pair(straight(normed[...], weight[:, cut(k, 256)]))

    @pl.loop(0, 2)
    def _(k):
        value[:, cut(k, 256)] = straight(normed[...], weight[:, cut(k + 6, 256)]).astype(jnp.bfloat16)

    bias = mask_bias(seg_col[...], seg_row[...])
    lse[...] = jnp.zeros_like(lse)
    lane = lax.broadcasted_iota(jnp.int32, (TOK_DEV, 128), 1)

    @pl.loop(0, 4)
    def _(p):
        queries = turned[:, cut(p, 256)]
        keys = turned[:, pl.ds(pl.multiple_of(1024 + p * 128, 128), 128)]
        values = value[:, cut(p, 128)]
        done, logs = [], lse[...]
        for h in range(4):
            side = slice(h // 2 * 64, h // 2 * 64 + 64)
            s = across(queries[:, h * 64 : h * 64 + 64], keys[:, side]) * SCORE_SCALE + bias
            top = jnp.max(s, axis=1, keepdims=True)
            e = jnp.exp(s - top)
            total = jnp.sum(e, axis=1, keepdims=True)
            prob = (e / total).astype(jnp.bfloat16)
            done.append(straight(prob, values[:, side]))
            logs = jnp.where(lane == p * 4 + h, top + jnp.log(total), logs)
        lse[...] = logs
        out[:, cut(p, 256)] = jnp.concatenate(done, axis=1).astype(jnp.bfloat16)

    keep = valid[...]

    @pl.loop(0, 4)
    def _(k):
        branch = straight(out[...], weight_out[:, cut(k, 256)])
        hidden[:, cut(k, 256)] = tok[:, cut(k, 256)].astype(jnp.float32) + keep * branch

    x = hidden[...]
    scale = lax.rsqrt(jnp.mean(x * x, axis=1, keepdims=True) + epsilon)
    normed_second[...] = (x * scale * second_gain[...]).astype(jnp.bfloat16)


def expert_body(held, x0, x1, grads, router, gate_up, down, lanes, *outs):
    x, inner_out, acts_out, logit_out, mixed, grad_x = outs[held:]
    x[:TOK_DEV, :] = x0[...]
    x[TOK_DEV:, :] = x1[...]
    logits = straight(x[...], router[...])
    routed = grads[:, D:].astype(jnp.float32) > 0.5
    logits = jnp.where(routed, logits, -1e30)
    terms = jnp.where(routed, jnp.exp(logits - jnp.max(logits, axis=1, keepdims=True)), 0.0)
    combine = terms / jnp.sum(terms, axis=1, keepdims=True)
    high = combine.astype(jnp.bfloat16)
    low = (combine - high.astype(jnp.float32)).astype(jnp.bfloat16)
    grad_gates = jnp.zeros(combine.shape, jnp.float32)
    for t in range(3):
        cols, cols_up = slice(t * 256, t * 256 + 256), slice(WIDE + t * 256, WIDE + t * 256 + 256)
        gate = straight(x[...], gate_up[:, cols])
        up = straight(x[...], gate_up[:, cols_up])
        spread = straight(high, lanes[:, cols]) + straight(low, lanes[:, cols])
        grad_down = across(grads[:, :D], down[cols, :])
        sig = 1.0 / (1.0 + jnp.exp(-gate))
        silu = gate * sig
        inner = (silu * up).astype(jnp.bfloat16).astype(jnp.float32)
        inner_out[:, cols] = (inner * spread).astype(jnp.bfloat16)
        grad_inner = grad_down * spread
        acts_out[:, cols] = (grad_inner * up * sig * (1.0 + gate * (1.0 - sig))).astype(jnp.bfloat16)
        acts_out[:, cols_up] = (grad_inner * silu).astype(jnp.bfloat16)
        product = inner * grad_down
        product_high = product.astype(jnp.bfloat16)
        product_low = (product - product_high.astype(jnp.float32)).astype(jnp.bfloat16)
        grad_gates += across(product_high, lanes[:, cols]) + across(product_low, lanes[:, cols])
    grad_logits = combine * (grad_gates - jnp.sum(combine * grad_gates, axis=1, keepdims=True))
    logit_out[...] = grad_logits.astype(jnp.bfloat16)

    @pl.loop(0, 4)
    def _(k):
        back = across(acts_out[...], gate_up[cut(k, 256), :])
        back += across(logit_out[...], router[cut(k, 256), :])
        grad_x[:, cut(k, 256)] = back.astype(jnp.bfloat16)
        mixed[:, cut(k, 256)] = straight(inner_out[...], down[:, cut(k, 256)]).astype(jnp.bfloat16)


def hidden_grad_body(dy, hidden, cot, gain, valid, weight, grad_hidden, branch, grad_att, gain_grad):
    x, d = hidden[...], dy[...]
    scale = lax.rsqrt(jnp.mean(x * x, axis=1, keepdims=True) + epsilon)
    gain_grad[...] = jnp.sum(d * x * scale, axis=0, keepdims=True)
    g = d * gain[...]
    dx = scale * g - x * scale * scale * scale * jnp.mean(g * x, axis=1, keepdims=True)
    total = cot[...].astype(jnp.float32) + dx
    grad_hidden[...] = total
    branch[...] = (valid[...] * total).astype(jnp.bfloat16)

    @pl.loop(0, 4)
    def _(k):
        grad_att[:, cut(k, 256)] = across(branch[...], weight[cut(k, 256), :]).astype(jnp.bfloat16)


def attend_grad_body(
    tok, gain, cosine, sine_part, seg_col, seg_row, weight, turned, value, lse, grad_att, grad_hidden,
    grad_query, grad_key_value, grad_tok, gain_grad, grad_normed,
):
    bias = mask_bias(seg_col[...], seg_row[...])
    cos, sin = cosine[...], -sine_part[...]
    lane = lax.broadcasted_iota(jnp.int32, (TOK_DEV, 128), 1)

    @pl.loop(0, 4)
    def _(p):
        queries = turned[:, cut(p, 256)]
        keys = turned[:, pl.ds(pl.multiple_of(1024 + p * 128, 128), 128)]
        values = value[:, cut(p, 128)]
        grads = grad_att[:, cut(p, 256)]
        for_query, for_key, for_value = [], [0.0, 0.0], [0.0, 0.0]
        for h in range(4):
            side = slice(h // 2 * 64, h // 2 * 64 + 64)
            own = slice(h * 64, h * 64 + 64)
            log_total = jnp.sum(jnp.where(lane == p * 4 + h, lse[...], 0.0), axis=1, keepdims=True)
            prob = jnp.exp(across(queries[:, own], keys[:, side]) * SCORE_SCALE + bias - log_total)
            grad_prob = across(grads[:, own], values[:, side])
            for_value[h // 2] += down_rows(prob.astype(jnp.bfloat16), grads[:, own])
            row_dot = jnp.sum(prob * grad_prob, axis=1, keepdims=True)
            grad_scores = (prob * (grad_prob - row_dot)).astype(jnp.bfloat16)
            for_query.append(straight(grad_scores, keys[:, side]) * SCORE_SCALE)
            for_key[h // 2] += down_rows(grad_scores, queries[:, own]) * SCORE_SCALE
        q = jnp.concatenate(for_query, axis=1)
        q = jnp.concatenate([turn(q[:, :128], cos, sin), turn(q[:, 128:], cos, sin)], axis=1)
        grad_query[:, cut(p, 256)] = q.astype(jnp.bfloat16)
        k = turn(jnp.concatenate(for_key, axis=1), cos, sin)
        grad_key_value[:, cut(p, 128)] = k.astype(jnp.bfloat16)
        v = jnp.concatenate(for_value, axis=1)
        grad_key_value[:, pl.ds(pl.multiple_of(512 + p * 128, 128), 128)] = v.astype(jnp.bfloat16)

    @pl.loop(0, 4)
    def _(k):
        back = across(grad_query[...], weight[cut(k, 256), :D])
        grad_normed[:, cut(k, 256)] = back + across(grad_key_value[...], weight[cut(k, 256), D:])

    x, d = tok[...].astype(jnp.float32), grad_normed[...]
    scale = lax.rsqrt(jnp.mean(x * x, axis=1, keepdims=True) + epsilon)
    gain_grad[...] = jnp.sum(d * x * scale, axis=0, keepdims=True)
    g = d * gain[...]
    dx = scale * g - x * scale * scale * scale * jnp.mean(g * x, axis=1, keepdims=True)
    grad_tok[...] = (grad_hidden[...] + dx).astype(jnp.bfloat16)


def shards(
    tokens,
    sequence_lengths,
    expert_index,
    cotangent,
    query_weight,
    key_weight,
    value_weight,
    output_weight,
    attention_gain,
    router_weight,
    mixture_gain,
    gate_weight,
    up_weight,
    down_weight,
):
    bfloat = jnp.bfloat16
    single = jnp.float32
    c = lax.axis_index("core")
    small = jnp.concatenate(
        [router_weight, jnp.zeros((8, 114), bfloat), attention_gain[:, None], mixture_gain[:, None]], axis=1
    )
    attention_full = lax.all_gather(
        jnp.concatenate([query_weight, key_weight, value_weight, output_weight, small], axis=1),
        ALL, axis=0, tiled=True,
    )
    gains = attention_full[:, 3198:].astype(single).T
    attn_gain_full, mix_gain_full = gains[:1], gains[1:]

    segment, position, valid_slot = seq_layout(sequence_lengths[0])
    seg_col, seg_row = segment[:, None], segment[None, :]
    valid_rows = valid_slot.astype(single)[:, None]
    cosine, sine_part = rope_tables(position)
    pick = jnp.any(
        expert_index[:, :, None] == jnp.arange(128, dtype=jnp.int32)[None, None, :], axis=1
    ).astype(bfloat)
    early = group_gather(jnp.concatenate([cotangent * valid_rows.astype(bfloat), pick], axis=1))
    early = jnp.concatenate([early[i] for i in (0, 1, 2, 3, 6, 7, 4, 5)], axis=0)
    order = column_order().astype(bfloat)
    spread = spread_order().astype(bfloat)
    gate_up = jnp.concatenate([gate_weight, up_weight], axis=0).reshape(24 * 8, FF)
    gate_up = jnp.dot(gate_up, order, preferred_element_type=single).astype(bfloat)
    gate_up = gate_up.reshape(24, 8, 8, 64).transpose(2, 1, 0, 3).reshape(4, 2, 8, 2 * WIDE)
    gate_up = group_exchange(gate_up).reshape(128, WIDE)
    gate_up = jnp.dot(gate_up, spread, preferred_element_type=single).astype(bfloat).reshape(64, 2 * WIDE)
    share = jnp.concatenate([gate_up, down_packed(down_weight.reshape(1, 48, D))], axis=1)
    share = lax.all_gather(share, ("y", "x"), axis=0, tiled=True)
    down_full = down_unpacked(share[:, 2 * WIDE :])
    lanes = expert_lanes().astype(bfloat)

    normed_first, turned, value_rows, attended, lse, hidden, normed_second = kernel_call(
        attend_body,
        [
            ((256, D), bfloat), ((256, 1536), bfloat), ((256, 512), bfloat), ((256, D), bfloat),
            ((256, 128), single), ((256, D), single), ((256, D), bfloat),
        ],
        in_specs=[ALL_OF] * 9 + [QKV_PART, OUT_PART],
        flops=3 * 10**9, moved=20 * 10**6,
    )(
        tokens, attn_gain_full, mix_gain_full, cosine, sine_part, seg_col, seg_row, valid_rows, lanes,
        attention_full, attention_full,
    )

    saved = []

    def experts(k, block, block_other):
        outs = [
            ((2048, D), bfloat), ((2048, WIDE), bfloat), ((2048, 2 * WIDE), bfloat), ((2048, 128), bfloat),
            ((512, D), bfloat), ((512, D), bfloat),
        ]
        rows_of = lambda width: pl.BlockSpec((512, width), lambda i: (k, 0))
        specs = [ALL_OF, ALL_OF, rows_of(D + 128), ROUTER_PART, GATE_UP_PART, ALL_OF, ALL_OF]
        result = kernel_call(
            functools.partial(expert_body, len(saved)),
            outs,
            in_specs=specs + [pl.BlockSpec(memory_space=pl.ANY)] * len(saved),
            out_specs=[rows_of(D), rows_of(WIDE), rows_of(2 * WIDE), rows_of(128), ALL_OF, ALL_OF],
            input_output_aliases={7 + i: i for i in range(len(saved))},
            flops=20 * 10**9, moved=20 * 10**6,
        )(block, block_other, early, attention_full, share, down_full, lanes, *saved)
        saved[:] = result[:4]
        both = result[5]
        other = shift(both[TOK_DEV:], "core", 1)
        return result[4], add_low(both[:TOK_DEV], other)

    near_other = shift(normed_second, "core", 1)
    above = shift(normed_second, "z", 1)
    below = shift(normed_second, "z", -1)
    mixed_own, back_own = experts(0, normed_second, near_other)
    above, below, back_own = lax.optimization_barrier((above, below, back_own))
    below_other = shift(below, "core", 1)
    above_other = shift(above, "core", 1)
    far = jnp.concatenate([shift(above[:128], "z", 1), shift(below[128:], "z", -1)], axis=0)
    mixed_below, back_below = experts(1, below, below_other)
    far, back_below = lax.optimization_barrier((far, back_below))
    far_other = shift(far, "core", 1)
    mixed_above, back_above = experts(2, above, above_other)
    mixed_far, back_far = experts(3, far, far_other)
    grad_normed_second = direct_sum((back_own, back_below, back_far, back_above), "z")
    rows, inner_scaled, grad_acts, grad_logits, back_far = lax.optimization_barrier((*saved, back_far))
    mixed, grad_normed_second = lax.optimization_barrier(
        ((mixed_own, mixed_below, mixed_far, mixed_above), grad_normed_second)
    )

    grad_hidden, grad_branch, grad_attended, mixture_gain_grad = kernel_call(
        hidden_grad_body,
        [((256, D), single), ((256, D), bfloat), ((256, D), bfloat), ((1, D), single)],
        in_specs=[ALL_OF] * 5 + [OUT_PART],
        flops=10**9, moved=6 * 10**6,
    )(grad_normed_second, hidden, cotangent, mix_gain_full, valid_rows, attention_full)
    grad_query, grad_key_value, grad_tokens, attention_gain_grad = kernel_call(
        attend_grad_body,
        [((256, D), bfloat), ((256, D), bfloat), ((256, D), bfloat), ((1, D), single)],
        in_specs=[ALL_OF] * 6 + [QKV_PART] + [ALL_OF] * 5,
        scratch=[pltpu.VMEM((256, D), single)],
        flops=3 * 10**9, moved=12 * 10**6,
    )(
        tokens, attn_gain_full, cosine, sine_part, seg_col, seg_row, attention_full, turned, value_rows, lse,
        grad_attended, grad_hidden,
    )

    gate_up_grad = down_rows(rows, grad_acts).astype(bfloat)
    down_grad = down_rows(inner_scaled, early[:, :D]).astype(bfloat).reshape(16, 48, D)
    router_grad = down_rows(rows, grad_logits)
    owned = jnp.concatenate([gate_up_grad, down_packed(down_grad)], axis=1)
    owned = lax.psum_scatter(owned, ("y", "x"), scatter_dimension=0, tiled=True).astype(single)
    down_owned = down_unpacked(owned[:, 2 * WIDE :]).reshape(12, 4, D)
    owned = owned[:, : 2 * WIDE].reshape(128, WIDE)
    exact = lax.Precision.HIGHEST
    owned = jnp.dot(owned, spread.T.astype(single), preferred_element_type=single, precision=exact)
    owned = group_exchange(owned.reshape(4, 2, 8, 2 * WIDE)).reshape(8, 8, 24, 64).transpose(2, 1, 0, 3).reshape(24 * 8, FF)
    owned = jnp.dot(owned, order.T.astype(single), preferred_element_type=single, precision=exact)
    owned = owned.reshape(2, EXPERTS, 8, FF)
    gate_owned, up_owned = owned[0], owned[1]

    other = shift(jnp.concatenate([m[TOK_DEV:] for m in mixed], axis=0), "core", 1)
    mixture = direct_sum(
        [add_low(m[:TOK_DEV], other[k * TOK_DEV : (k + 1) * TOK_DEV]) for k, m in enumerate(mixed)], "z"
    )
    layer_out = (hidden + valid_rows * mixture).astype(bfloat)

    normed_both = jnp.concatenate([normed_first, shift(normed_first, "core", 1)], axis=0)
    attended_both = jnp.concatenate([attended, shift(attended, "core", 1)], axis=0)

    def both_cores(left, right):
        mine, sent = jnp.where(c == 0, left, right), jnp.where(c == 0, right, left)
        return jnp.concatenate([mine, shift(sent, "core", 1)], axis=0)

    branch_both = both_cores(grad_branch[:, : D // 2], grad_branch[:, D // 2 :])
    output_grad = down_rows(attended_both, branch_both).astype(bfloat).reshape(4, 4, 4, 16, D // 2)
    output_sum = torus_sum(output_grad, "xzy", "yxz", direct_sum)
    qkv_both = both_cores(grad_query, grad_key_value)
    qkv_grad = down_rows(normed_both, qkv_both).astype(bfloat)
    small_grad = jnp.concatenate(
        [router_grad[:, :126], attention_gain_grad.T, mixture_gain_grad.T], axis=1
    ).astype(bfloat)
    small_grad = add_low(small_grad, shift(small_grad, "core", 1))
    first = torus_sum(qkv_grad[:, :512].reshape(4, 4, 4, 16, 512), "yxz", "yxz", direct_sum)
    second = jnp.concatenate([qkv_grad[:, 512:], small_grad], axis=1).reshape(4, 4, 4, 16, 640)
    second = torus_sum(second, "zxy", "yxz", direct_sum)
    half = jnp.concatenate([first, second, output_sum], axis=1)
    mine = lax.dynamic_slice_in_dim(half, c * 8, 8, axis=0)
    got = shift(lax.dynamic_slice_in_dim(half, (1 - c) * 8, 8, axis=0), "core", 1)
    left, right = jnp.where(c == 0, mine, got), jnp.where(c == 0, got, mine)
    return (
        layer_out,
        grad_tokens,
        left[:, :D],
        right[:, :512],
        right[:, 512:D],
        jnp.concatenate([left[:, 1152:], right[:, 1152:]], axis=1),
        left[:, 1150],
        left[:, 1024:1036],
        left[:, 1151],
        gate_owned,
        up_owned,
        down_owned,
    )


def solution(mesh):
    mesh = Mesh(mesh.devices.reshape(4, 4, 4, 2), ALL)
    rows, line, inner = P(ALL, None), P(ALL), P(None, ALL, None)
    return jax.shard_map(
        shards,
        mesh=mesh,
        in_specs=(rows,) * 8 + (line, rows, line) + (inner,) * 3,
        out_specs=(rows,) * 6 + (line, rows, line) + (inner,) * 3,
        check_vma=False,
    )
```

```python
import functools
import math

import jax
import jax.numpy as jnp
from jax import lax
from jax.experimental import pallas as pl
from jax.experimental.pallas import tpu as pltpu
from jax.sharding import Mesh, PartitionSpec as P

D = 1024
HEADS = 16
KV_HEADS = 8
HEAD_DIM = 64
EXPERTS = 12
TOP = 8
SEQ_DEV = 4
TOK_DEV = 256
FF = 512
WIDE = EXPERTS * 64
ALL = ("y", "x", "z", "core")


epsilon = 1e-06
rope_base = 10000.0
SCORE_SCALE = 1.0 / math.sqrt(HEAD_DIM)


def shift(v, axis, s):
    n = lax.axis_size(axis)
    return lax.ppermute(v, axis, [(i, (i + s) % n) for i in range(n)])


def add_low(*terms):
    return sum(a.astype(jnp.float32) for a in terms).astype(jnp.bfloat16)


def group_gather(v):
    half = v.shape[0] // 2
    above = shift(v, "z", 1)
    below = shift(v, "z", -1)
    far = jnp.concatenate([shift(above[:half], "z", 1), shift(below[half:], "z", -1)], axis=0)
    blocks = []
    for block in (v, below, far, above):
        blocks += [block, shift(block, "core", 1)]
    return blocks


def ring_sum(parts, axis):
    half = parts[2].shape[0] // 2
    front = shift(parts[2][:half], axis, 1)
    back = shift(parts[2][half:], axis, -1)
    ahead = jnp.concatenate([add_low(parts[1][:half], front), parts[1][half:]], axis=0)
    behind = jnp.concatenate([parts[3][:half], add_low(parts[3][half:], back)], axis=0)
    return sum(a.astype(jnp.float32) for a in (parts[0], shift(ahead, axis, 1), shift(behind, axis, -1)))


def direct_sum(parts, axis):
    terms = (parts[0], shift(parts[1], axis, 1), shift(parts[2], axis, 2), shift(parts[3], axis, -1))
    return sum(a.astype(jnp.float32) for a in terms)


def group_sum(blocks, how=ring_sum):
    other = [shift(b, "core", 1) for b in blocks[1::2]]
    return how([add_low(a, b) for a, b in zip(blocks[::2], other)], "z")


def axis_sum(v, axis, dim, how):
    me = lax.axis_index(axis)
    parts = [lax.dynamic_index_in_dim(v, (me + k) % 4, dim, keepdims=False) for k in range(4)]
    return how(parts, axis)


def torus_sum(v, order, axes, how=ring_sum):
    axes = list(axes)
    for i, axis in enumerate(order):
        v = axis_sum(v, axis, axes.index(axis), how)
        axes.remove(axis)
        if i < len(order) - 1:
            v = v.astype(jnp.bfloat16)
    return v


def axis_gather(v, axis):
    me = lax.axis_index(axis)
    parts = [v, shift(v, axis, -1), shift(v, axis, 2), shift(v, axis, 1)]
    line = jnp.stack(parts + parts[:3], axis=0)
    return lax.dynamic_slice_in_dim(line, (4 - me) % 4, 4, axis=0)


def down_packed(v):
    n = v.shape[0]
    rest = v[:, :, 768:].reshape(n, 3, 16, 256).swapaxes(1, 2).reshape(n, 16, 768)
    return jnp.concatenate([v[:, :, :768], rest], axis=1).reshape(n * 64, 768)


def down_unpacked(v):
    v = v.reshape(-1, 64, 768)
    rest = v[:, 48:].reshape(-1, 16, 3, 256).swapaxes(1, 2).reshape(-1, 48, 256)
    return jnp.concatenate([v[:, :48], rest], axis=2).reshape(-1, D)


def group_exchange(v):
    z, c = lax.axis_index("z"), lax.axis_index("core")
    keep = lax.dynamic_index_in_dim(v, c, 1, keepdims=False)
    got = shift(lax.dynamic_index_in_dim(v, 1 - c, 1, keepdims=False), "core", 1)
    first = jnp.where(c == 0, keep, got)
    second = jnp.where(c == 0, got, keep)
    both = jnp.stack([first, second], axis=1)
    parts = [lax.dynamic_index_in_dim(both, (z + k) % 4, 0, keepdims=False) for k in range(4)]
    came = [parts[0]] + [shift(parts[k], "z", k) for k in (1, 2, 3)]
    line = jnp.stack([came[0], came[3], came[2], came[1]] * 2, axis=0)
    return lax.dynamic_slice_in_dim(line, (4 - z) % 4, 4, axis=0)


def column_order():
    column = lax.broadcasted_iota(jnp.int32, (FF, FF), 1)
    feature = lax.broadcasted_iota(jnp.int32, (FF, FF), 0)
    return feature == (column // 4 % 16) * 32 + (column // 64) * 4 + column % 4


def spread_order():
    column = lax.broadcasted_iota(jnp.int32, (WIDE, WIDE), 1)
    feature = lax.broadcasted_iota(jnp.int32, (WIDE, WIDE), 0)
    return feature == (column % 48) // 4 * 64 + column // 48 * 4 + column % 4


def expert_lanes():
    expert = (lax.broadcasted_iota(jnp.int32, (128, WIDE), 1) % 48) // 4
    return expert == lax.broadcasted_iota(jnp.int32, (128, WIDE), 0)


def seq_layout(lengths):
    ends_at = jnp.cumsum(lengths)
    starts_at = ends_at - lengths
    slot_index = jnp.arange(TOK_DEV, dtype=jnp.int32)
    segment = jnp.sum((slot_index[:, None] >= ends_at[None, :]).astype(jnp.int32), axis=1)
    owners = segment[:, None] == jnp.arange(SEQ_DEV, dtype=jnp.int32)[None, :]
    begins = jnp.sum(jnp.where(owners, starts_at[None, :], 0), axis=1)
    return (segment, slot_index - begins, segment < SEQ_DEV)


def rope_tables(position):
    half_size = HEAD_DIM // 2
    frequency = rope_base ** (-2.0 * jnp.arange(half_size, dtype=jnp.float32) / HEAD_DIM)
    angles = position.astype(jnp.float32)[:, None] * frequency[None, :]
    cosine, sine_part = jnp.cos(angles), jnp.sin(angles)
    return (
        jnp.concatenate([cosine] * 4, axis=1),
        jnp.concatenate([-sine_part, sine_part] * 2, axis=1),
    )


def across(a, b):
    return lax.dot_general(a, b, (((1,), (1,)), ((), ())), preferred_element_type=jnp.float32)


def down_rows(a, b):
    return lax.dot_general(a, b, (((0,), (0,)), ((), ())), preferred_element_type=jnp.float32)


def straight(a, b):
    return jnp.dot(a, b, preferred_element_type=jnp.float32)


def turn(x, cosine, sine_part):
    lane = lax.broadcasted_iota(jnp.int32, x.shape, 1) % HEAD_DIM
    other = jnp.where(lane < HEAD_DIM // 2, pltpu.roll(x, 96, 1), pltpu.roll(x, 32, 1))
    return x * cosine + other * sine_part


def cut(k, size):
    return pl.ds(pl.multiple_of(k * size, size), size)


ALL_OF = pl.BlockSpec(memory_space=pltpu.VMEM)
QKV_PART = pl.BlockSpec((D, 2 * D), lambda i: (0, 0))
OUT_PART = pl.BlockSpec((D, D), lambda i: (0, 2))
CORNER = pl.BlockSpec((16, 128), lambda i: (0, 0))
ROUTER_PART = pl.BlockSpec((D, 128), lambda i: (0, 24))
GATE_UP_PART = pl.BlockSpec((D, 2 * WIDE), lambda i: (0, 0))


def kernel_call(body, outs, scratch=(), flops=0, moved=0, **more):
    return pl.pallas_call(
        body,
        out_shape=[jax.ShapeDtypeStruct(shape, kind) for shape, kind in outs],
        grid=(1,),
        scratch_shapes=list(scratch),
        compiler_params=pltpu.CompilerParams(vmem_limit_bytes=60 * 1024 * 1024),
        cost_estimate=pl.CostEstimate(flops=flops, bytes_accessed=moved, transcendentals=0),
        **more,
    )


def mask_bias(seg_col, seg_row):
    row = lax.broadcasted_iota(jnp.int32, (TOK_DEV, TOK_DEV), 0)
    column = lax.broadcasted_iota(jnp.int32, (TOK_DEV, TOK_DEV), 1)
    return jnp.where((seg_col == seg_row) & (column <= row), 0.0, -1e30)


def attend_body(
    tok, gain, second_gain, cosine, sine_part, seg_col, seg_row, valid, weight, weight_out,
    normed, turned, value, out, lse, hidden, normed_second,
):
    x = tok[...].astype(jnp.float32)
    scale = lax.rsqrt(jnp.mean(x * x, axis=1, keepdims=True) + epsilon)
    normed[...] = (x * scale * gain[...]).astype(jnp.bfloat16)
    cos, sin = cosine[...], sine_part[...]

    def turned_pair(raw):
        both = [turn(raw[:, :128], cos, sin), turn(raw[:, 128:], cos, sin)]
        return jnp.concatenate(both, axis=1).astype(jnp.bfloat16)

    @pl.loop(0, 6)
    def _(k):
        turned[:, cut(k, 256)] = turned_pair(straight(normed[...], weight[:, cut(k, 256)]))

    @pl.loop(0, 2)
    def _(k):
        value[:, cut(k, 256)] = straight(normed[...], weight[:, cut(k + 6, 256)]).astype(jnp.bfloat16)

    bias = mask_bias(seg_col[...], seg_row[...])
    lse[...] = jnp.zeros_like(lse)
    lane = lax.broadcasted_iota(jnp.int32, (TOK_DEV, 128), 1)

    @pl.loop(0, 4)
    def _(p):
        queries = turned[:, cut(p, 256)]
        keys = turned[:, pl.ds(pl.multiple_of(1024 + p * 128, 128), 128)]
        values = value[:, cut(p, 128)]
        done, logs = [], lse[...]
        for h in range(4):
            side = slice(h // 2 * 64, h // 2 * 64 + 64)
            s = across(queries[:, h * 64 : h * 64 + 64], keys[:, side]) * SCORE_SCALE + bias
            top = jnp.max(s, axis=1, keepdims=True)
            e = jnp.exp(s - top)
            total = jnp.sum(e, axis=1, keepdims=True)
            prob = (e / total).astype(jnp.bfloat16)
            done.append(straight(prob, values[:, side]))
            logs = jnp.where(lane == p * 4 + h, top + jnp.log(total), logs)
        lse[...] = logs
        out[:, cut(p, 256)] = jnp.concatenate(done, axis=1).astype(jnp.bfloat16)

    keep = valid[...]

    @pl.loop(0, 4)
    def _(k):
        branch = straight(out[...], weight_out[:, cut(k, 256)])
        hidden[:, cut(k, 256)] = tok[:, cut(k, 256)].astype(jnp.float32) + keep * branch

    x = hidden[...]
    scale = lax.rsqrt(jnp.mean(x * x, axis=1, keepdims=True) + epsilon)
    normed_second[...] = (x * scale * second_gain[...]).astype(jnp.bfloat16)


def expert_body(held, x0, x1, grads, router, gate_up, down, lanes, *outs):
    x, inner_out, acts_out, logit_out, mixed, grad_x = outs[held:]
    x[:TOK_DEV, :] = x0[...]
    x[TOK_DEV:, :] = x1[...]
    logits = straight(x[...], router[...])
    routed = grads[:, D:].astype(jnp.float32) > 0.5
    logits = jnp.where(routed, logits, -1e30)
    terms = jnp.where(routed, jnp.exp(logits - jnp.max(logits, axis=1, keepdims=True)), 0.0)
    combine = terms / jnp.sum(terms, axis=1, keepdims=True)
    high = combine.astype(jnp.bfloat16)
    low = (combine - high.astype(jnp.float32)).astype(jnp.bfloat16)
    grad_gates = jnp.zeros(combine.shape, jnp.float32)
    for t in range(3):
        cols, cols_up = slice(t * 256, t * 256 + 256), slice(WIDE + t * 256, WIDE + t * 256 + 256)
        gate = straight(x[...], gate_up[:, cols])
        up = straight(x[...], gate_up[:, cols_up])
        spread = straight(high, lanes[:, cols]) + straight(low, lanes[:, cols])
        grad_down = across(grads[:, :D], down[cols, :])
        sig = 1.0 / (1.0 + jnp.exp(-gate))
        silu = gate * sig
        inner = (silu * up).astype(jnp.bfloat16).astype(jnp.float32)
        inner_out[:, cols] = (inner * spread).astype(jnp.bfloat16)
        grad_inner = grad_down * spread
        acts_out[:, cols] = (grad_inner * up * sig * (1.0 + gate * (1.0 - sig))).astype(jnp.bfloat16)
        acts_out[:, cols_up] = (grad_inner * silu).astype(jnp.bfloat16)
        product = inner * grad_down
        product_high = product.astype(jnp.bfloat16)
        product_low = (product - product_high.astype(jnp.float32)).astype(jnp.bfloat16)
        grad_gates += across(product_high, lanes[:, cols]) + across(product_low, lanes[:, cols])
    grad_logits = combine * (grad_gates - jnp.sum(combine * grad_gates, axis=1, keepdims=True))
    logit_out[...] = grad_logits.astype(jnp.bfloat16)

    @pl.loop(0, 4)
    def _(k):
        back = across(acts_out[...], gate_up[cut(k, 256), :])
        back += across(logit_out[...], router[cut(k, 256), :])
        grad_x[:, cut(k, 256)] = back.astype(jnp.bfloat16)
        mixed[:, cut(k, 256)] = straight(inner_out[...], down[:, cut(k, 256)]).astype(jnp.bfloat16)


def hidden_grad_body(dy, hidden, cot, gain, valid, weight, grad_hidden, branch, grad_att, gain_grad):
    x, d = hidden[...], dy[...]
    scale = lax.rsqrt(jnp.mean(x * x, axis=1, keepdims=True) + epsilon)
    gain_grad[...] = jnp.sum(d * x * scale, axis=0, keepdims=True)
    g = d * gain[...]
    dx = scale * g - x * scale * scale * scale * jnp.mean(g * x, axis=1, keepdims=True)
    total = cot[...].astype(jnp.float32) + dx
    grad_hidden[...] = total
    branch[...] = (valid[...] * total).astype(jnp.bfloat16)

    @pl.loop(0, 4)
    def _(k):
        grad_att[:, cut(k, 256)] = across(branch[...], weight[cut(k, 256), :]).astype(jnp.bfloat16)


def attend_grad_body(
    tok, gain, cosine, sine_part, seg_col, seg_row, weight, turned, value, lse, grad_att, grad_hidden,
    hidden, valid, mixed, mixed_ahead, mixed_behind,
    grad_query, grad_key_value, grad_tok, gain_grad, layer_out, grad_normed,
):
    mixture = sum(m[...].astype(jnp.float32) for m in (mixed, mixed_ahead, mixed_behind))
    layer_out[...] = (hidden[...] + valid[...] * mixture).astype(jnp.bfloat16)
    bias = mask_bias(seg_col[...], seg_row[...])
    cos, sin = cosine[...], -sine_part[...]
    lane = lax.broadcasted_iota(jnp.int32, (TOK_DEV, 128), 1)

    @pl.loop(0, 4)
    def _(p):
        queries = turned[:, cut(p, 256)]
        keys = turned[:, pl.ds(pl.multiple_of(1024 + p * 128, 128), 128)]
        values = value[:, cut(p, 128)]
        grads = grad_att[:, cut(p, 256)]
        for_query, for_key, for_value = [], [0.0, 0.0], [0.0, 0.0]
        for h in range(4):
            side = slice(h // 2 * 64, h // 2 * 64 + 64)
            own = slice(h * 64, h * 64 + 64)
            log_total = jnp.sum(jnp.where(lane == p * 4 + h, lse[...], 0.0), axis=1, keepdims=True)
            prob = jnp.exp(across(queries[:, own], keys[:, side]) * SCORE_SCALE + bias - log_total)
            grad_prob = across(grads[:, own], values[:, side])
            for_value[h // 2] += down_rows(prob.astype(jnp.bfloat16), grads[:, own])
            row_dot = jnp.sum(prob * grad_prob, axis=1, keepdims=True)
            grad_scores = (prob * (grad_prob - row_dot)).astype(jnp.bfloat16)
            for_query.append(straight(grad_scores, keys[:, side]) * SCORE_SCALE)
            for_key[h // 2] += down_rows(grad_scores, queries[:, own]) * SCORE_SCALE
        q = jnp.concatenate(for_query, axis=1)
        q = jnp.concatenate([turn(q[:, :128], cos, sin), turn(q[:, 128:], cos, sin)], axis=1)
        grad_query[:, cut(p, 256)] = q.astype(jnp.bfloat16)
        k = turn(jnp.concatenate(for_key, axis=1), cos, sin)
        grad_key_value[:, cut(p, 128)] = k.astype(jnp.bfloat16)
        v = jnp.concatenate(for_value, axis=1)
        grad_key_value[:, pl.ds(pl.multiple_of(512 + p * 128, 128), 128)] = v.astype(jnp.bfloat16)

    @pl.loop(0, 4)
    def _(k):
        back = across(grad_query[...], weight[cut(k, 256), :D])
        grad_normed[:, cut(k, 256)] = back + across(grad_key_value[...], weight[cut(k, 256), D:])

    x, d = tok[...].astype(jnp.float32), grad_normed[...]
    scale = lax.rsqrt(jnp.mean(x * x, axis=1, keepdims=True) + epsilon)
    gain_grad[...] = jnp.sum(d * x * scale, axis=0, keepdims=True)
    g = d * gain[...]
    dx = scale * g - x * scale * scale * scale * jnp.mean(g * x, axis=1, keepdims=True)
    grad_tok[...] = (grad_hidden[...] + dx).astype(jnp.bfloat16)


def shards(
    tokens,
    sequence_lengths,
    expert_index,
    cotangent,
    query_weight,
    key_weight,
    value_weight,
    output_weight,
    attention_gain,
    router_weight,
    mixture_gain,
    gate_weight,
    up_weight,
    down_weight,
):
    bfloat = jnp.bfloat16
    single = jnp.float32
    c = lax.axis_index("core")
    small = jnp.concatenate(
        [router_weight, jnp.zeros((8, 114), bfloat), attention_gain[:, None], mixture_gain[:, None]], axis=1
    )
    attention_full = lax.all_gather(
        jnp.concatenate([query_weight, key_weight, value_weight, output_weight, small], axis=1),
        ALL, axis=0, tiled=True,
    )
    gains = attention_full[:, 3198:].astype(single).T
    attn_gain_full, mix_gain_full = gains[:1], gains[1:]

    segment, position, valid_slot = seq_layout(sequence_lengths[0])
    seg_col, seg_row = segment[:, None], segment[None, :]
    valid_rows = valid_slot.astype(single)[:, None]
    cosine, sine_part = rope_tables(position)
    pick = jnp.any(
        expert_index[:, :, None] == jnp.arange(128, dtype=jnp.int32)[None, None, :], axis=1
    ).astype(bfloat)
    early = group_gather(jnp.concatenate([cotangent * valid_rows.astype(bfloat), pick], axis=1))
    early = jnp.concatenate([early[i] for i in (4, 5, 2, 3, 6, 7, 0, 1)], axis=0)
    order = column_order().astype(bfloat)
    spread = spread_order().astype(bfloat)
    gate_up = jnp.concatenate([gate_weight, up_weight], axis=0).reshape(24 * 8, FF)
    gate_up = jnp.dot(gate_up, order, preferred_element_type=single).astype(bfloat)
    gate_up = gate_up.reshape(24, 8, 8, 64).transpose(2, 1, 0, 3).reshape(4, 2, 8, 2 * WIDE)
    gate_up = group_exchange(gate_up).reshape(128, WIDE)
    gate_up = jnp.dot(gate_up, spread, preferred_element_type=single).astype(bfloat).reshape(64, 2 * WIDE)
    share = jnp.concatenate([gate_up, down_packed(down_weight.reshape(1, 48, D))], axis=1)
    share = lax.all_gather(share, ("y", "x"), axis=0, tiled=True)
    down_full = down_unpacked(share[:, 2 * WIDE :])
    lanes = expert_lanes().astype(bfloat)

    normed_first, turned, value_rows, attended, lse, hidden, normed_second = kernel_call(
        attend_body,
        [
            ((256, D), bfloat), ((256, 1536), bfloat), ((256, 512), bfloat), ((256, D), bfloat),
            ((256, 128), single), ((256, D), single), ((256, D), bfloat),
        ],
        in_specs=[ALL_OF] * 8 + [QKV_PART, OUT_PART],
        flops=3 * 10**9, moved=20 * 10**6,
    )(
        tokens, attn_gain_full, mix_gain_full, cosine, sine_part, seg_col, seg_row, valid_rows,
        attention_full, attention_full,
    )

    saved = []

    def experts(k, block, block_other, after=()):
        outs = [
            ((2048, D), bfloat), ((2048, WIDE), bfloat), ((2048, 2 * WIDE), bfloat), ((2048, 128), bfloat),
            ((512, D), bfloat), ((512, D), bfloat),
        ]
        rows_of = lambda width: pl.BlockSpec((512, width), lambda i: (k, 0))
        specs = [ALL_OF, ALL_OF, rows_of(D + 128), ROUTER_PART, GATE_UP_PART, ALL_OF, ALL_OF]
        result = kernel_call(
            functools.partial(expert_body, len(after) + len(saved)),
            outs,
            in_specs=specs + [CORNER] * len(after) + [pl.BlockSpec(memory_space=pl.ANY)] * len(saved),
            out_specs=[rows_of(D), rows_of(WIDE), rows_of(2 * WIDE), rows_of(128), ALL_OF, ALL_OF],
            input_output_aliases={7 + len(after) + i: i for i in range(len(saved))},
            flops=20 * 10**9, moved=20 * 10**6,
        )(block, block_other, early, attention_full, share, down_full, lanes, *after, *saved)
        saved[:] = result[:4]
        return [
            add_low(both[:TOK_DEV], shift(both[TOK_DEV:], "core", 1)) for both in (result[5], result[4])
        ]

    blocks = group_gather(normed_second)
    half = TOK_DEV // 2
    far, far_mixed = experts(0, blocks[4], blocks[5])
    near_below, mixed_below = experts(1, blocks[2], blocks[3])
    front, back = shift(far[:half], "z", 1), shift(far[half:], "z", -1)
    near_above, mixed_above = experts(2, blocks[6], blocks[7], [far])
    own, own_mixed = experts(3, blocks[0], blocks[1], [front, back])

    def send_near(below, above, front, back):
        below = jnp.concatenate([add_low(below[:half], front), below[half:]], axis=0)
        above = jnp.concatenate([above[:half], add_low(above[half:], back)], axis=0)
        return shift(below, "z", 1), shift(above, "z", -1)

    ahead, behind = send_near(near_below, near_above, front, back)
    grad_normed_second = sum(v.astype(single) for v in (own, ahead, behind))
    far_mixed, grad_normed_second = lax.optimization_barrier((far_mixed, grad_normed_second))
    front, back = shift(far_mixed[:half], "z", 1), shift(far_mixed[half:], "z", -1)
    mixed_ahead, mixed_behind = send_near(mixed_below, mixed_above, front, back)

    grad_hidden, grad_branch, grad_attended, mixture_gain_grad = kernel_call(
        hidden_grad_body,
        [((256, D), single), ((256, D), bfloat), ((256, D), bfloat), ((1, D), single)],
        in_specs=[ALL_OF] * 5 + [OUT_PART],
        flops=10**9, moved=6 * 10**6,
    )(grad_normed_second, hidden, cotangent, mix_gain_full, valid_rows, attention_full)
    rows, inner_scaled, grad_acts, grad_logits, _ = lax.optimization_barrier((*saved, grad_attended))
    grad_query, grad_key_value, grad_tokens, attention_gain_grad, layer_out = kernel_call(
        attend_grad_body,
        [((256, D), bfloat), ((256, D), bfloat), ((256, D), bfloat), ((1, D), single), ((256, D), bfloat)],
        in_specs=[ALL_OF] * 6 + [QKV_PART] + [ALL_OF] * 10,
        scratch=[pltpu.VMEM((256, D), single)],
        flops=3 * 10**9, moved=12 * 10**6,
    )(
        tokens, attn_gain_full, cosine, sine_part, seg_col, seg_row, attention_full, turned, value_rows, lse,
        grad_attended, grad_hidden, hidden, valid_rows, own_mixed, mixed_ahead, mixed_behind,
    )

    gate_up_grad = down_rows(rows, grad_acts).astype(bfloat)
    down_grad = down_rows(inner_scaled, early[:, :D]).astype(bfloat).reshape(16, 48, D)
    router_grad = down_rows(rows, grad_logits)
    owned = jnp.concatenate([gate_up_grad, down_packed(down_grad)], axis=1)
    owned = lax.psum_scatter(owned, ("y", "x"), scatter_dimension=0, tiled=True).astype(single)
    down_owned = down_unpacked(owned[:, 2 * WIDE :]).reshape(12, 4, D)
    owned = owned[:, : 2 * WIDE].reshape(128, WIDE)
    exact = lax.Precision.HIGHEST
    gathered = jnp.dot(owned, spread.T.astype(single), preferred_element_type=single, precision=exact)
    gathered = group_exchange(gathered.reshape(4, 2, 8, 2 * WIDE))

    normed_both = jnp.concatenate([normed_first, shift(normed_first, "core", 1)], axis=0)
    attended_both = jnp.concatenate([attended, shift(attended, "core", 1)], axis=0)

    def both_cores(left, right):
        mine, sent = jnp.where(c == 0, left, right), jnp.where(c == 0, right, left)
        return jnp.concatenate([mine, shift(sent, "core", 1)], axis=0)

    branch_both = both_cores(grad_branch[:, : D // 2], grad_branch[:, D // 2 :])
    output_grad = down_rows(attended_both, branch_both).astype(bfloat).reshape(4, 4, 4, 16, D // 2)
    output_sum = torus_sum(output_grad, "xzy", "yxz", direct_sum)
    qkv_both = both_cores(grad_query, grad_key_value)
    qkv_grad = down_rows(normed_both, qkv_both).astype(bfloat)
    small_grad = jnp.concatenate(
        [router_grad[:, :126], attention_gain_grad.T, mixture_gain_grad.T], axis=1
    ).astype(bfloat)
    small_grad = add_low(small_grad, shift(small_grad, "core", 1))
    first = torus_sum(qkv_grad[:, :512].reshape(4, 4, 4, 16, 512), "yxz", "yxz", direct_sum)
    second = jnp.concatenate([qkv_grad[:, 512:], small_grad], axis=1).reshape(4, 4, 4, 16, 640)
    second = torus_sum(second, "zx", "yxz", direct_sum).astype(bfloat)
    second, gathered = lax.optimization_barrier((second, gathered))
    second = torus_sum(second, "y", "y", direct_sum)
    owned = gathered.reshape(8, 8, 24, 64).transpose(2, 1, 0, 3).reshape(24 * 8, FF)
    owned = jnp.dot(owned, order.T.astype(single), preferred_element_type=single, precision=exact)
    owned = owned.reshape(2, EXPERTS, 8, FF)
    gate_owned, up_owned = owned[0], owned[1]
    half = jnp.concatenate([first, second, output_sum], axis=1)
    mine = lax.dynamic_slice_in_dim(half, c * 8, 8, axis=0)
    got = shift(lax.dynamic_slice_in_dim(half, (1 - c) * 8, 8, axis=0), "core", 1)
    left, right = jnp.where(c == 0, mine, got), jnp.where(c == 0, got, mine)
    return (
        layer_out,
        grad_tokens,
        left[:, :D],
        right[:, :512],
        right[:, 512:D],
        jnp.concatenate([left[:, 1152:], right[:, 1152:]], axis=1),
        left[:, 1150],
        left[:, 1024:1036],
        left[:, 1151],
        gate_owned,
        up_owned,
        down_owned,
    )


def solution(mesh):
    mesh = Mesh(mesh.devices.reshape(4, 4, 4, 2), ALL)
    rows, line, inner = P(ALL, None), P(ALL), P(None, ALL, None)
    return jax.shard_map(
        shards,
        mesh=mesh,
        in_specs=(rows,) * 8 + (line, rows, line) + (inner,) * 3,
        out_specs=(rows,) * 6 + (line, rows, line) + (inner,) * 3,
        check_vma=False,
    )
```

```python
import functools
import math

import jax
import jax.numpy as jnp
from jax import lax
from jax.experimental import pallas as pl
from jax.experimental.pallas import tpu as pltpu
from jax.sharding import Mesh, PartitionSpec as P

D = 1024
HEADS = 16
KV_HEADS = 8
HEAD_DIM = 64
EXPERTS = 12
TOP = 8
SEQ_DEV = 4
TOK_DEV = 256
FF = 512
WIDE = EXPERTS * 64
ALL = ("y", "x", "z", "core")


epsilon = 1e-06
rope_base = 10000.0
SCORE_SCALE = 1.0 / math.sqrt(HEAD_DIM)


def shift(v, axis, s):
    n = lax.axis_size(axis)
    return lax.ppermute(v, axis, [(i, (i + s) % n) for i in range(n)])


def add_low(*terms):
    return sum(a.astype(jnp.float32) for a in terms).astype(jnp.bfloat16)


def group_gather(v):
    half = v.shape[0] // 2
    above = shift(v, "z", 1)
    below = shift(v, "z", -1)
    far = jnp.concatenate([shift(above[:half], "z", 1), shift(below[half:], "z", -1)], axis=0)
    blocks = []
    for block in (v, below, far, above):
        blocks += [block, shift(block, "core", 1)]
    return blocks


def ring_sum(parts, axis):
    half = parts[2].shape[0] // 2
    front = shift(parts[2][:half], axis, 1)
    back = shift(parts[2][half:], axis, -1)
    ahead = jnp.concatenate([add_low(parts[1][:half], front), parts[1][half:]], axis=0)
    behind = jnp.concatenate([parts[3][:half], add_low(parts[3][half:], back)], axis=0)
    return sum(a.astype(jnp.float32) for a in (parts[0], shift(ahead, axis, 1), shift(behind, axis, -1)))


def direct_sum(parts, axis):
    terms = (parts[0], shift(parts[1], axis, 1), shift(parts[2], axis, 2), shift(parts[3], axis, -1))
    return sum(a.astype(jnp.float32) for a in terms)


def group_sum(blocks, how=ring_sum):
    other = [shift(b, "core", 1) for b in blocks[1::2]]
    return how([add_low(a, b) for a, b in zip(blocks[::2], other)], "z")


def axis_sum(v, axis, dim, how):
    me = lax.axis_index(axis)
    parts = [lax.dynamic_index_in_dim(v, (me + k) % 4, dim, keepdims=False) for k in range(4)]
    return how(parts, axis)


def torus_sum(v, order, axes, how=ring_sum):
    axes = list(axes)
    for i, axis in enumerate(order):
        v = axis_sum(v, axis, axes.index(axis), how)
        axes.remove(axis)
        if i < len(order) - 1:
            v = v.astype(jnp.bfloat16)
    return v


def axis_gather(v, axis):
    me = lax.axis_index(axis)
    parts = [v, shift(v, axis, -1), shift(v, axis, 2), shift(v, axis, 1)]
    line = jnp.stack(parts + parts[:3], axis=0)
    return lax.dynamic_slice_in_dim(line, (4 - me) % 4, 4, axis=0)


def down_packed(v):
    n = v.shape[0]
    rest = v[:, :, 768:].reshape(n, 3, 16, 256).swapaxes(1, 2).reshape(n, 16, 768)
    return jnp.concatenate([v[:, :, :768], rest], axis=1).reshape(n * 64, 768)


def down_unpacked(v):
    v = v.reshape(-1, 64, 768)
    rest = v[:, 48:].reshape(-1, 16, 3, 256).swapaxes(1, 2).reshape(-1, 48, 256)
    return jnp.concatenate([v[:, :48], rest], axis=2).reshape(-1, D)


def group_exchange(v):
    z, c = lax.axis_index("z"), lax.axis_index("core")
    keep = lax.dynamic_index_in_dim(v, c, 1, keepdims=False)
    got = shift(lax.dynamic_index_in_dim(v, 1 - c, 1, keepdims=False), "core", 1)
    first = jnp.where(c == 0, keep, got)
    second = jnp.where(c == 0, got, keep)
    both = jnp.stack([first, second], axis=1)
    parts = [lax.dynamic_index_in_dim(both, (z + k) % 4, 0, keepdims=False) for k in range(4)]
    came = [parts[0]] + [shift(parts[k], "z", k) for k in (1, 2, 3)]
    line = jnp.stack([came[0], came[3], came[2], came[1]] * 2, axis=0)
    return lax.dynamic_slice_in_dim(line, (4 - z) % 4, 4, axis=0)


def column_order():
    column = lax.broadcasted_iota(jnp.int32, (FF, FF), 1)
    feature = lax.broadcasted_iota(jnp.int32, (FF, FF), 0)
    return feature == (column // 4 % 16) * 32 + (column // 64) * 4 + column % 4


def spread_order():
    column = lax.broadcasted_iota(jnp.int32, (WIDE, WIDE), 1)
    feature = lax.broadcasted_iota(jnp.int32, (WIDE, WIDE), 0)
    return feature == (column % 48) // 4 * 64 + column // 48 * 4 + column % 4


def expert_lanes():
    expert = (lax.broadcasted_iota(jnp.int32, (128, WIDE), 1) % 48) // 4
    return expert == lax.broadcasted_iota(jnp.int32, (128, WIDE), 0)


def seq_layout(lengths):
    ends_at = jnp.cumsum(lengths)
    starts_at = ends_at - lengths
    slot_index = jnp.arange(TOK_DEV, dtype=jnp.int32)
    segment = jnp.sum((slot_index[:, None] >= ends_at[None, :]).astype(jnp.int32), axis=1)
    owners = segment[:, None] == jnp.arange(SEQ_DEV, dtype=jnp.int32)[None, :]
    begins = jnp.sum(jnp.where(owners, starts_at[None, :], 0), axis=1)
    return (segment, slot_index - begins, segment < SEQ_DEV)


def rope_tables(position):
    half_size = HEAD_DIM // 2
    frequency = rope_base ** (-2.0 * jnp.arange(half_size, dtype=jnp.float32) / HEAD_DIM)
    angles = position.astype(jnp.float32)[:, None] * frequency[None, :]
    cosine, sine_part = jnp.cos(angles), jnp.sin(angles)
    return (
        jnp.concatenate([cosine] * 4, axis=1),
        jnp.concatenate([-sine_part, sine_part] * 2, axis=1),
    )


def across(a, b):
    return lax.dot_general(a, b, (((1,), (1,)), ((), ())), preferred_element_type=jnp.float32)


def down_rows(a, b):
    return lax.dot_general(a, b, (((0,), (0,)), ((), ())), preferred_element_type=jnp.float32)


def straight(a, b):
    return jnp.dot(a, b, preferred_element_type=jnp.float32)


def turn(x, cosine, sine_part):
    lane = lax.broadcasted_iota(jnp.int32, x.shape, 1) % HEAD_DIM
    other = jnp.where(lane < HEAD_DIM // 2, pltpu.roll(x, 96, 1), pltpu.roll(x, 32, 1))
    return x * cosine + other * sine_part


def cut(k, size):
    return pl.ds(pl.multiple_of(k * size, size), size)


ALL_OF = pl.BlockSpec(memory_space=pltpu.VMEM)
QKV_PART = pl.BlockSpec((D, 2 * D), lambda i: (0, 0))
OUT_PART = pl.BlockSpec((D, D), lambda i: (0, 2))
CORNER = pl.BlockSpec((16, 128), lambda i: (0, 0))
ROUTER_PART = pl.BlockSpec((D, 128), lambda i: (0, 24))
GATE_UP_PART = pl.BlockSpec((D, 2 * WIDE), lambda i: (0, 0))


def kernel_call(body, outs, scratch=(), flops=0, moved=0, **more):
    return pl.pallas_call(
        body,
        out_shape=[jax.ShapeDtypeStruct(shape, kind) for shape, kind in outs],
        grid=(1,),
        scratch_shapes=list(scratch),
        compiler_params=pltpu.CompilerParams(vmem_limit_bytes=60 * 1024 * 1024),
        cost_estimate=pl.CostEstimate(flops=flops, bytes_accessed=moved, transcendentals=0),
        **more,
    )


def mask_bias(seg_col, seg_row):
    row = lax.broadcasted_iota(jnp.int32, (TOK_DEV, TOK_DEV), 0)
    column = lax.broadcasted_iota(jnp.int32, (TOK_DEV, TOK_DEV), 1)
    return jnp.where((seg_col == seg_row) & (column <= row), 0.0, -1e30)


def attend_body(
    tok, gain, second_gain, cosine, sine_part, seg_col, seg_row, valid, weight, weight_out,
    normed, turned, value, out, lse, hidden, normed_second,
):
    x = tok[...].astype(jnp.float32)
    scale = lax.rsqrt(jnp.mean(x * x, axis=1, keepdims=True) + epsilon)
    normed[...] = (x * scale * gain[...]).astype(jnp.bfloat16)
    cos, sin = cosine[...], sine_part[...]

    def turned_pair(raw):
        both = [turn(raw[:, :128], cos, sin), turn(raw[:, 128:], cos, sin)]
        return jnp.concatenate(both, axis=1).astype(jnp.bfloat16)

    @pl.loop(0, 6)
    def _(k):
        turned[:, cut(k, 256)] = turned_pair(straight(normed[...], weight[:, cut(k, 256)]))

    @pl.loop(0, 2)
    def _(k):
        value[:, cut(k, 256)] = straight(normed[...], weight[:, cut(k + 6, 256)]).astype(jnp.bfloat16)

    bias = mask_bias(seg_col[...], seg_row[...])
    lse[...] = jnp.zeros_like(lse)
    lane = lax.broadcasted_iota(jnp.int32, (TOK_DEV, 128), 1)

    @pl.loop(0, 4)
    def _(p):
        queries = turned[:, cut(p, 256)]
        keys = turned[:, pl.ds(pl.multiple_of(1024 + p * 128, 128), 128)]
        values = value[:, cut(p, 128)]
        done, logs = [], lse[...]
        for h in range(4):
            side = slice(h // 2 * 64, h // 2 * 64 + 64)
            s = across(queries[:, h * 64 : h * 64 + 64], keys[:, side]) * SCORE_SCALE + bias
            top = jnp.max(s, axis=1, keepdims=True)
            e = jnp.exp(s - top)
            total = jnp.sum(e, axis=1, keepdims=True)
            prob = (e / total).astype(jnp.bfloat16)
            done.append(straight(prob, values[:, side]))
            logs = jnp.where(lane == p * 4 + h, top + jnp.log(total), logs)
        lse[...] = logs
        out[:, cut(p, 256)] = jnp.concatenate(done, axis=1).astype(jnp.bfloat16)

    keep = valid[...]

    @pl.loop(0, 4)
    def _(k):
        branch = straight(out[...], weight_out[:, cut(k, 256)])
        hidden[:, cut(k, 256)] = tok[:, cut(k, 256)].astype(jnp.float32) + keep * branch

    x = hidden[...]
    scale = lax.rsqrt(jnp.mean(x * x, axis=1, keepdims=True) + epsilon)
    normed_second[...] = (x * scale * second_gain[...]).astype(jnp.bfloat16)


def expert_body(held, x0, x1, grads, router, gate_up, down, lanes, *outs):
    x, inner_out, acts_out, logit_out, mixed, grad_x = outs[held:]
    x[:TOK_DEV, :] = x0[...]
    x[TOK_DEV:, :] = x1[...]
    logits = straight(x[...], router[...])
    routed = grads[:, D:].astype(jnp.float32) > 0.5
    logits = jnp.where(routed, logits, -1e30)
    terms = jnp.where(routed, jnp.exp(logits - jnp.max(logits, axis=1, keepdims=True)), 0.0)
    combine = terms / jnp.sum(terms, axis=1, keepdims=True)
    high = combine.astype(jnp.bfloat16)
    low = (combine - high.astype(jnp.float32)).astype(jnp.bfloat16)
    grad_gates = jnp.zeros(combine.shape, jnp.float32)
    for t in range(3):
        cols, cols_up = slice(t * 256, t * 256 + 256), slice(WIDE + t * 256, WIDE + t * 256 + 256)
        gate = straight(x[...], gate_up[:, cols])
        up = straight(x[...], gate_up[:, cols_up])
        spread = straight(high, lanes[:, cols]) + straight(low, lanes[:, cols])
        grad_down = across(grads[:, :D], down[cols, :])
        sig = 1.0 / (1.0 + jnp.exp(-gate))
        silu = gate * sig
        inner = (silu * up).astype(jnp.bfloat16).astype(jnp.float32)
        inner_out[:, cols] = (inner * spread).astype(jnp.bfloat16)
        grad_inner = grad_down * spread
        acts_out[:, cols] = (grad_inner * up * sig * (1.0 + gate * (1.0 - sig))).astype(jnp.bfloat16)
        acts_out[:, cols_up] = (grad_inner * silu).astype(jnp.bfloat16)
        product = inner * grad_down
        product_high = product.astype(jnp.bfloat16)
        product_low = (product - product_high.astype(jnp.float32)).astype(jnp.bfloat16)
        grad_gates += across(product_high, lanes[:, cols]) + across(product_low, lanes[:, cols])
    grad_logits = combine * (grad_gates - jnp.sum(combine * grad_gates, axis=1, keepdims=True))
    logit_out[...] = grad_logits.astype(jnp.bfloat16)

    @pl.loop(0, 4)
    def _(k):
        back = across(acts_out[...], gate_up[cut(k, 256), :])
        back += across(logit_out[...], router[cut(k, 256), :])
        grad_x[:, cut(k, 256)] = back.astype(jnp.bfloat16)
        mixed[:, cut(k, 256)] = straight(inner_out[...], down[:, cut(k, 256)]).astype(jnp.bfloat16)


def hidden_grad_body(dy, hidden, cot, gain, valid, weight, grad_hidden, branch, grad_att, gain_grad):
    x, d = hidden[...], dy[...]
    scale = lax.rsqrt(jnp.mean(x * x, axis=1, keepdims=True) + epsilon)
    gain_grad[...] = jnp.sum(d * x * scale, axis=0, keepdims=True)
    g = d * gain[...]
    dx = scale * g - x * scale * scale * scale * jnp.mean(g * x, axis=1, keepdims=True)
    total = cot[...].astype(jnp.float32) + dx
    grad_hidden[...] = total
    branch[...] = (valid[...] * total).astype(jnp.bfloat16)

    @pl.loop(0, 4)
    def _(k):
        grad_att[:, cut(k, 256)] = across(branch[...], weight[cut(k, 256), :]).astype(jnp.bfloat16)


def attend_grad_body(
    tok, gain, cosine, sine_part, seg_col, seg_row, weight, turned, value, lse, grad_att, grad_hidden,
    grad_query, grad_key_value, grad_tok, gain_grad, grad_normed,
):
    bias = mask_bias(seg_col[...], seg_row[...])
    cos, sin = cosine[...], -sine_part[...]
    lane = lax.broadcasted_iota(jnp.int32, (TOK_DEV, 128), 1)

    @pl.loop(0, 4)
    def _(p):
        queries = turned[:, cut(p, 256)]
        keys = turned[:, pl.ds(pl.multiple_of(1024 + p * 128, 128), 128)]
        values = value[:, cut(p, 128)]
        grads = grad_att[:, cut(p, 256)]
        for_query, for_key, for_value = [], [0.0, 0.0], [0.0, 0.0]
        for h in range(4):
            side = slice(h // 2 * 64, h // 2 * 64 + 64)
            own = slice(h * 64, h * 64 + 64)
            log_total = jnp.sum(jnp.where(lane == p * 4 + h, lse[...], 0.0), axis=1, keepdims=True)
            prob = jnp.exp(across(queries[:, own], keys[:, side]) * SCORE_SCALE + bias - log_total)
            grad_prob = across(grads[:, own], values[:, side])
            for_value[h // 2] += down_rows(prob.astype(jnp.bfloat16), grads[:, own])
            row_dot = jnp.sum(prob * grad_prob, axis=1, keepdims=True)
            grad_scores = (prob * (grad_prob - row_dot)).astype(jnp.bfloat16)
            for_query.append(straight(grad_scores, keys[:, side]) * SCORE_SCALE)
            for_key[h // 2] += down_rows(grad_scores, queries[:, own]) * SCORE_SCALE
        q = jnp.concatenate(for_query, axis=1)
        q = jnp.concatenate([turn(q[:, :128], cos, sin), turn(q[:, 128:], cos, sin)], axis=1)
        grad_query[:, cut(p, 256)] = q.astype(jnp.bfloat16)
        k = turn(jnp.concatenate(for_key, axis=1), cos, sin)
        grad_key_value[:, cut(p, 128)] = k.astype(jnp.bfloat16)
        v = jnp.concatenate(for_value, axis=1)
        grad_key_value[:, pl.ds(pl.multiple_of(512 + p * 128, 128), 128)] = v.astype(jnp.bfloat16)

    @pl.loop(0, 4)
    def _(k):
        back = across(grad_query[...], weight[cut(k, 256), :D])
        grad_normed[:, cut(k, 256)] = back + across(grad_key_value[...], weight[cut(k, 256), D:])

    x, d = tok[...].astype(jnp.float32), grad_normed[...]
    scale = lax.rsqrt(jnp.mean(x * x, axis=1, keepdims=True) + epsilon)
    gain_grad[...] = jnp.sum(d * x * scale, axis=0, keepdims=True)
    g = d * gain[...]
    dx = scale * g - x * scale * scale * scale * jnp.mean(g * x, axis=1, keepdims=True)
    grad_tok[...] = (grad_hidden[...] + dx).astype(jnp.bfloat16)


def shards(
    tokens,
    sequence_lengths,
    expert_index,
    cotangent,
    query_weight,
    key_weight,
    value_weight,
    output_weight,
    attention_gain,
    router_weight,
    mixture_gain,
    gate_weight,
    up_weight,
    down_weight,
):
    bfloat = jnp.bfloat16
    single = jnp.float32
    c = lax.axis_index("core")
    small = jnp.concatenate(
        [router_weight, jnp.zeros((8, 114), bfloat), attention_gain[:, None], mixture_gain[:, None]], axis=1
    )
    attention_full = lax.all_gather(
        jnp.concatenate([query_weight, key_weight, value_weight, output_weight, small], axis=1),
        ALL, axis=0, tiled=True,
    )
    gains = attention_full[:, 3198:].astype(single).T
    attn_gain_full, mix_gain_full = gains[:1], gains[1:]

    segment, position, valid_slot = seq_layout(sequence_lengths[0])
    seg_col, seg_row = segment[:, None], segment[None, :]
    valid_rows = valid_slot.astype(single)[:, None]
    cosine, sine_part = rope_tables(position)
    pick = jnp.any(
        expert_index[:, :, None] == jnp.arange(128, dtype=jnp.int32)[None, None, :], axis=1
    ).astype(bfloat)
    early = group_gather(jnp.concatenate([cotangent * valid_rows.astype(bfloat), pick], axis=1))
    early = jnp.concatenate([early[i] for i in (4, 5, 2, 3, 6, 7, 0, 1)], axis=0)
    order = column_order().astype(bfloat)
    spread = spread_order().astype(bfloat)
    gate_up = jnp.concatenate([gate_weight, up_weight], axis=0).reshape(24 * 8, FF)
    gate_up = jnp.dot(gate_up, order, preferred_element_type=single).astype(bfloat)
    gate_up = gate_up.reshape(24, 8, 8, 64).transpose(2, 1, 0, 3).reshape(4, 2, 8, 2 * WIDE)
    gate_up = group_exchange(gate_up).reshape(128, WIDE)
    gate_up = jnp.dot(gate_up, spread, preferred_element_type=single).astype(bfloat).reshape(64, 2 * WIDE)
    share = jnp.concatenate([gate_up, down_packed(down_weight.reshape(1, 48, D))], axis=1)
    share = lax.all_gather(share, ("y", "x"), axis=0, tiled=True)
    down_full = down_unpacked(share[:, 2 * WIDE :])
    lanes = expert_lanes().astype(bfloat)

    normed_first, turned, value_rows, attended, lse, hidden, normed_second = kernel_call(
        attend_body,
        [
            ((256, D), bfloat), ((256, 1536), bfloat), ((256, 512), bfloat), ((256, D), bfloat),
            ((256, 128), single), ((256, D), single), ((256, D), bfloat),
        ],
        in_specs=[ALL_OF] * 8 + [QKV_PART, OUT_PART],
        flops=3 * 10**9, moved=20 * 10**6,
    )(
        tokens, attn_gain_full, mix_gain_full, cosine, sine_part, seg_col, seg_row, valid_rows,
        attention_full, attention_full,
    )

    saved = []

    def experts(k, block, block_other, after=()):
        outs = [
            ((2048, D), bfloat), ((2048, WIDE), bfloat), ((2048, 2 * WIDE), bfloat), ((2048, 128), bfloat),
            ((512, D), bfloat), ((512, D), bfloat),
        ]
        rows_of = lambda width: pl.BlockSpec((512, width), lambda i: (k, 0))
        specs = [ALL_OF, ALL_OF, rows_of(D + 128), ROUTER_PART, GATE_UP_PART, ALL_OF, ALL_OF]
        result = kernel_call(
            functools.partial(expert_body, len(after) + len(saved)),
            outs,
            in_specs=specs + [CORNER] * len(after) + [pl.BlockSpec(memory_space=pl.ANY)] * len(saved),
            out_specs=[rows_of(D), rows_of(WIDE), rows_of(2 * WIDE), rows_of(128), ALL_OF, ALL_OF],
            input_output_aliases={7 + len(after) + i: i for i in range(len(saved))},
            flops=20 * 10**9, moved=20 * 10**6,
        )(block, block_other, early, attention_full, share, down_full, lanes, *after, *saved)
        saved[:] = result[:4]
        return [
            add_low(both[:TOK_DEV], shift(both[TOK_DEV:], "core", 1)) for both in (result[5], result[4])
        ]

    blocks = group_gather(normed_second)
    half = TOK_DEV // 2
    far, far_mixed = experts(0, blocks[4], blocks[5])
    near_below, mixed_below = experts(1, blocks[2], blocks[3])
    front, back = shift(far[:half], "z", 1), shift(far[half:], "z", -1)
    near_above, mixed_above = experts(2, blocks[6], blocks[7], [far])
    own, own_mixed = experts(3, blocks[0], blocks[1], [near_below])

    def with_far(below, above, front, back):
        below = jnp.concatenate([add_low(below[:half], front), below[half:]], axis=0)
        return below, jnp.concatenate([above[:half], add_low(above[half:], back)], axis=0)

    near_below, near_above = with_far(near_below, near_above, front, back)
    ahead, behind = shift(near_below, "z", 1), shift(near_above, "z", -1)
    rows, inner_scaled, grad_acts, grad_logits, _, _ = lax.optimization_barrier((*saved, near_below, near_above))
    grad_normed_second = sum(v.astype(single) for v in (own, ahead, behind))
    far_mixed, grad_normed_second = lax.optimization_barrier((far_mixed, grad_normed_second))
    front, back = shift(far_mixed[:half], "z", 1), shift(far_mixed[half:], "z", -1)

    grad_hidden, grad_branch, grad_attended, mixture_gain_grad = kernel_call(
        hidden_grad_body,
        [((256, D), single), ((256, D), bfloat), ((256, D), bfloat), ((1, D), single)],
        in_specs=[ALL_OF] * 5 + [OUT_PART],
        flops=10**9, moved=6 * 10**6,
    )(grad_normed_second, hidden, cotangent, mix_gain_full, valid_rows, attention_full)
    grad_query, grad_key_value, grad_tokens, attention_gain_grad = kernel_call(
        attend_grad_body,
        [((256, D), bfloat), ((256, D), bfloat), ((256, D), bfloat), ((1, D), single)],
        in_specs=[ALL_OF] * 6 + [QKV_PART] + [ALL_OF] * 5,
        scratch=[pltpu.VMEM((256, D), single)],
        flops=3 * 10**9, moved=12 * 10**6,
    )(
        tokens, attn_gain_full, cosine, sine_part, seg_col, seg_row, attention_full, turned, value_rows, lse,
        grad_attended, grad_hidden,
    )

    gate_up_grad = down_rows(rows, grad_acts).astype(bfloat)
    down_grad = down_rows(inner_scaled, early[:, :D]).astype(bfloat).reshape(16, 48, D)
    router_grad = down_rows(rows, grad_logits)
    owned = jnp.concatenate([gate_up_grad, down_packed(down_grad)], axis=1)
    owned = lax.psum_scatter(owned, ("y", "x"), scatter_dimension=0, tiled=True).astype(single)
    down_owned = down_unpacked(owned[:, 2 * WIDE :]).reshape(12, 4, D)
    owned = owned[:, : 2 * WIDE].reshape(128, WIDE)
    exact = lax.Precision.HIGHEST
    gathered = jnp.dot(owned, spread.T.astype(single), preferred_element_type=single, precision=exact)
    gathered = group_exchange(gathered.reshape(4, 2, 8, 2 * WIDE))

    normed_both = jnp.concatenate([normed_first, shift(normed_first, "core", 1)], axis=0)
    attended_both = jnp.concatenate([attended, shift(attended, "core", 1)], axis=0)

    def both_cores(left, right):
        mine, sent = jnp.where(c == 0, left, right), jnp.where(c == 0, right, left)
        return jnp.concatenate([mine, shift(sent, "core", 1)], axis=0)

    branch_both = both_cores(grad_branch[:, : D // 2], grad_branch[:, D // 2 :])
    output_grad = down_rows(attended_both, branch_both).astype(bfloat).reshape(4, 4, 4, 16, D // 2)
    output_sum = torus_sum(output_grad, "x", "yxz", direct_sum).astype(bfloat)
    output_sum, front, back, grad_query = lax.optimization_barrier((output_sum, front, back, grad_query))
    output_sum = torus_sum(output_sum, "zy", "yz", direct_sum)
    mixed_below, mixed_above = with_far(mixed_below, mixed_above, front, back)
    mixed_ahead, mixed_behind = shift(mixed_below, "z", 1), shift(mixed_above, "z", -1)
    mixture = sum(v.astype(single) for v in (own_mixed, mixed_ahead, mixed_behind))
    layer_out = (hidden + valid_rows * mixture).astype(bfloat)
    qkv_both = both_cores(grad_query, grad_key_value)
    qkv_grad = down_rows(normed_both, qkv_both).astype(bfloat)
    small_grad = jnp.concatenate(
        [router_grad[:, :126], attention_gain_grad.T, mixture_gain_grad.T], axis=1
    ).astype(bfloat)
    small_grad = add_low(small_grad, shift(small_grad, "core", 1))
    first = torus_sum(qkv_grad[:, :512].reshape(4, 4, 4, 16, 512), "yxz", "yxz", direct_sum)
    second = jnp.concatenate([qkv_grad[:, 512:], small_grad], axis=1).reshape(4, 4, 4, 16, 640)
    second = torus_sum(second, "zx", "yxz", direct_sum).astype(bfloat)
    second, gathered, layer_out = lax.optimization_barrier((second, gathered, layer_out))
    second = torus_sum(second, "y", "y", direct_sum)
    owned = gathered.reshape(8, 8, 24, 64).transpose(2, 1, 0, 3).reshape(24 * 8, FF)
    owned = jnp.dot(owned, order.T.astype(single), preferred_element_type=single, precision=exact)
    owned = owned.reshape(2, EXPERTS, 8, FF)
    gate_owned, up_owned = owned[0], owned[1]
    half = jnp.concatenate([first, second, output_sum], axis=1)
    mine = lax.dynamic_slice_in_dim(half, c * 8, 8, axis=0)
    got = shift(lax.dynamic_slice_in_dim(half, (1 - c) * 8, 8, axis=0), "core", 1)
    left, right = jnp.where(c == 0, mine, got), jnp.where(c == 0, got, mine)
    return (
        layer_out,
        grad_tokens,
        left[:, :D],
        right[:, :512],
        right[:, 512:D],
        jnp.concatenate([left[:, 1152:], right[:, 1152:]], axis=1),
        left[:, 1150],
        left[:, 1024:1036],
        left[:, 1151],
        gate_owned,
        up_owned,
        down_owned,
    )


def solution(mesh):
    mesh = Mesh(mesh.devices.reshape(4, 4, 4, 2), ALL)
    rows, line, inner = P(ALL, None), P(ALL), P(None, ALL, None)
    return jax.shard_map(
        shards,
        mesh=mesh,
        in_specs=(rows,) * 8 + (line, rows, line) + (inner,) * 3,
        out_specs=(rows,) * 6 + (line, rows, line) + (inner,) * 3,
        check_vma=False,
    )
```

```python
import functools
import math

import jax
import jax.numpy as jnp
from jax import lax
from jax.experimental import pallas as pl
from jax.experimental.pallas import tpu as pltpu
from jax.sharding import Mesh, PartitionSpec as P

D = 1024
HEADS = 16
KV_HEADS = 8
HEAD_DIM = 64
EXPERTS = 12
TOP = 8
SEQ_DEV = 4
TOK_DEV = 256
FF = 512
WIDE = EXPERTS * 64
ALL = ("y", "x", "z", "core")


epsilon = 1e-06
rope_base = 10000.0
SCORE_SCALE = 1.0 / math.sqrt(HEAD_DIM)


def shift(v, axis, s):
    n = lax.axis_size(axis)
    return lax.ppermute(v, axis, [(i, (i + s) % n) for i in range(n)])


def add_low(*terms):
    return sum(a.astype(jnp.float32) for a in terms).astype(jnp.bfloat16)


def group_gather(v):
    half = v.shape[0] // 2
    above = shift(v, "z", 1)
    below = shift(v, "z", -1)
    far = jnp.concatenate([shift(above[:half], "z", 1), shift(below[half:], "z", -1)], axis=0)
    blocks = []
    for block in (v, below, far, above):
        blocks += [block, shift(block, "core", 1)]
    return blocks


def ring_sum(parts, axis):
    half = parts[2].shape[0] // 2
    front = shift(parts[2][:half], axis, 1)
    back = shift(parts[2][half:], axis, -1)
    ahead = jnp.concatenate([add_low(parts[1][:half], front), parts[1][half:]], axis=0)
    behind = jnp.concatenate([parts[3][:half], add_low(parts[3][half:], back)], axis=0)
    return sum(a.astype(jnp.float32) for a in (parts[0], shift(ahead, axis, 1), shift(behind, axis, -1)))


def direct_sum(parts, axis):
    terms = (parts[0], shift(parts[1], axis, 1), shift(parts[2], axis, 2), shift(parts[3], axis, -1))
    return sum(a.astype(jnp.float32) for a in terms)


def group_sum(blocks, how=ring_sum):
    other = [shift(b, "core", 1) for b in blocks[1::2]]
    return how([add_low(a, b) for a, b in zip(blocks[::2], other)], "z")


def axis_sum(v, axis, dim, how):
    me = lax.axis_index(axis)
    parts = [lax.dynamic_index_in_dim(v, (me + k) % 4, dim, keepdims=False) for k in range(4)]
    return how(parts, axis)


def torus_sum(v, order, axes, how=ring_sum):
    axes = list(axes)
    for i, axis in enumerate(order):
        v = axis_sum(v, axis, axes.index(axis), how)
        axes.remove(axis)
        if i < len(order) - 1:
            v = v.astype(jnp.bfloat16)
    return v


def axis_gather(v, axis):
    me = lax.axis_index(axis)
    parts = [v, shift(v, axis, -1), shift(v, axis, 2), shift(v, axis, 1)]
    line = jnp.stack(parts + parts[:3], axis=0)
    return lax.dynamic_slice_in_dim(line, (4 - me) % 4, 4, axis=0)


def down_packed(v):
    n = v.shape[0]
    rest = v[:, :, 768:].reshape(n, 3, 16, 256).swapaxes(1, 2).reshape(n, 16, 768)
    return jnp.concatenate([v[:, :, :768], rest], axis=1).reshape(n * 64, 768)


def down_unpacked(v):
    v = v.reshape(-1, 64, 768)
    rest = v[:, 48:].reshape(-1, 16, 3, 256).swapaxes(1, 2).reshape(-1, 48, 256)
    return jnp.concatenate([v[:, :48], rest], axis=2).reshape(-1, D)


def group_exchange(v):
    z, c = lax.axis_index("z"), lax.axis_index("core")
    keep = lax.dynamic_index_in_dim(v, c, 1, keepdims=False)
    got = shift(lax.dynamic_index_in_dim(v, 1 - c, 1, keepdims=False), "core", 1)
    first = jnp.where(c == 0, keep, got)
    second = jnp.where(c == 0, got, keep)
    both = jnp.stack([first, second], axis=1)
    parts = [lax.dynamic_index_in_dim(both, (z + k) % 4, 0, keepdims=False) for k in range(4)]
    came = [parts[0]] + [shift(parts[k], "z", k) for k in (1, 2, 3)]
    line = jnp.stack([came[0], came[3], came[2], came[1]] * 2, axis=0)
    return lax.dynamic_slice_in_dim(line, (4 - z) % 4, 4, axis=0)


def column_order():
    column = lax.broadcasted_iota(jnp.int32, (FF, FF), 1)
    feature = lax.broadcasted_iota(jnp.int32, (FF, FF), 0)
    return feature == (column // 4 % 16) * 32 + (column // 64) * 4 + column % 4


def spread_order():
    column = lax.broadcasted_iota(jnp.int32, (WIDE, WIDE), 1)
    feature = lax.broadcasted_iota(jnp.int32, (WIDE, WIDE), 0)
    return feature == (column % 48) // 4 * 64 + column // 48 * 4 + column % 4


def expert_lanes():
    expert = (lax.broadcasted_iota(jnp.int32, (128, WIDE), 1) % 48) // 4
    return expert == lax.broadcasted_iota(jnp.int32, (128, WIDE), 0)


def seq_layout(lengths):
    ends_at = jnp.cumsum(lengths)
    starts_at = ends_at - lengths
    slot_index = jnp.arange(TOK_DEV, dtype=jnp.int32)
    segment = jnp.sum((slot_index[:, None] >= ends_at[None, :]).astype(jnp.int32), axis=1)
    owners = segment[:, None] == jnp.arange(SEQ_DEV, dtype=jnp.int32)[None, :]
    begins = jnp.sum(jnp.where(owners, starts_at[None, :], 0), axis=1)
    return (segment, slot_index - begins, segment < SEQ_DEV)


def rope_tables(position):
    half_size = HEAD_DIM // 2
    frequency = rope_base ** (-2.0 * jnp.arange(half_size, dtype=jnp.float32) / HEAD_DIM)
    angles = position.astype(jnp.float32)[:, None] * frequency[None, :]
    cosine, sine_part = jnp.cos(angles), jnp.sin(angles)
    return (
        jnp.concatenate([cosine] * 4, axis=1),
        jnp.concatenate([-sine_part, sine_part] * 2, axis=1),
    )


def across(a, b):
    return lax.dot_general(a, b, (((1,), (1,)), ((), ())), preferred_element_type=jnp.float32)


def down_rows(a, b):
    return lax.dot_general(a, b, (((0,), (0,)), ((), ())), preferred_element_type=jnp.float32)


def straight(a, b):
    return jnp.dot(a, b, preferred_element_type=jnp.float32)


def turn(x, cosine, sine_part):
    lane = lax.broadcasted_iota(jnp.int32, x.shape, 1) % HEAD_DIM
    other = jnp.where(lane < HEAD_DIM // 2, pltpu.roll(x, 96, 1), pltpu.roll(x, 32, 1))
    return x * cosine + other * sine_part


def cut(k, size):
    return pl.ds(pl.multiple_of(k * size, size), size)


ALL_OF = pl.BlockSpec(memory_space=pltpu.VMEM)
QKV_PART = pl.BlockSpec((D, 2 * D), lambda i: (0, 0))
OUT_PART = pl.BlockSpec((D, D), lambda i: (0, 2))
CORNER = pl.BlockSpec((16, 128), lambda i: (0, 0))
ROUTER_PART = pl.BlockSpec((D, 128), lambda i: (0, 24))
GATE_UP_PART = pl.BlockSpec((D, 2 * WIDE), lambda i: (0, 0))


def kernel_call(body, outs, scratch=(), flops=0, moved=0, **more):
    return pl.pallas_call(
        body,
        out_shape=[jax.ShapeDtypeStruct(shape, kind) for shape, kind in outs],
        grid=(1,),
        scratch_shapes=list(scratch),
        compiler_params=pltpu.CompilerParams(vmem_limit_bytes=60 * 1024 * 1024),
        cost_estimate=pl.CostEstimate(flops=flops, bytes_accessed=moved, transcendentals=0),
        **more,
    )


def mask_bias(seg_col, seg_row):
    row = lax.broadcasted_iota(jnp.int32, (TOK_DEV, TOK_DEV), 0)
    column = lax.broadcasted_iota(jnp.int32, (TOK_DEV, TOK_DEV), 1)
    return jnp.where((seg_col == seg_row) & (column <= row), 0.0, -1e30)


def attend_body(
    tok, gain, second_gain, cosine, sine_part, seg_col, seg_row, valid, weight, weight_out,
    normed, turned, value, out, lse, hidden, normed_second,
):
    x = tok[...].astype(jnp.float32)
    scale = lax.rsqrt(jnp.mean(x * x, axis=1, keepdims=True) + epsilon)
    normed[...] = (x * scale * gain[...]).astype(jnp.bfloat16)
    cos, sin = cosine[...], sine_part[...]

    def turned_pair(raw):
        both = [turn(raw[:, :128], cos, sin), turn(raw[:, 128:], cos, sin)]
        return jnp.concatenate(both, axis=1).astype(jnp.bfloat16)

    @pl.loop(0, 6)
    def _(k):
        turned[:, cut(k, 256)] = turned_pair(straight(normed[...], weight[:, cut(k, 256)]))

    @pl.loop(0, 2)
    def _(k):
        value[:, cut(k, 256)] = straight(normed[...], weight[:, cut(k + 6, 256)]).astype(jnp.bfloat16)

    bias = mask_bias(seg_col[...], seg_row[...])
    lse[...] = jnp.zeros_like(lse)
    lane = lax.broadcasted_iota(jnp.int32, (TOK_DEV, 128), 1)

    @pl.loop(0, 4)
    def _(p):
        queries = turned[:, cut(p, 256)]
        keys = turned[:, pl.ds(pl.multiple_of(1024 + p * 128, 128), 128)]
        values = value[:, cut(p, 128)]
        done, logs = [], lse[...]
        for h in range(4):
            side = slice(h // 2 * 64, h // 2 * 64 + 64)
            s = across(queries[:, h * 64 : h * 64 + 64], keys[:, side]) * SCORE_SCALE + bias
            top = jnp.max(s, axis=1, keepdims=True)
            e = jnp.exp(s - top)
            total = jnp.sum(e, axis=1, keepdims=True)
            prob = (e / total).astype(jnp.bfloat16)
            done.append(straight(prob, values[:, side]))
            logs = jnp.where(lane == p * 4 + h, top + jnp.log(total), logs)
        lse[...] = logs
        out[:, cut(p, 256)] = jnp.concatenate(done, axis=1).astype(jnp.bfloat16)

    keep = valid[...]

    @pl.loop(0, 4)
    def _(k):
        branch = straight(out[...], weight_out[:, cut(k, 256)])
        hidden[:, cut(k, 256)] = tok[:, cut(k, 256)].astype(jnp.float32) + keep * branch

    x = hidden[...]
    scale = lax.rsqrt(jnp.mean(x * x, axis=1, keepdims=True) + epsilon)
    normed_second[...] = (x * scale * second_gain[...]).astype(jnp.bfloat16)


def expert_body(held, x0, x1, grads, router, gate_up, down, lanes, *outs):
    x, inner_out, acts_out, logit_out, grad_x, grad_x_other, mixed, mixed_other = outs[held:]
    x[:TOK_DEV, :] = x0[...]
    x[TOK_DEV:, :] = x1[...]
    logits = straight(x[...], router[...])
    routed = grads[:, D:].astype(jnp.float32) > 0.5
    logits = jnp.where(routed, logits, -1e30)
    terms = jnp.where(routed, jnp.exp(logits - jnp.max(logits, axis=1, keepdims=True)), 0.0)
    combine = terms / jnp.sum(terms, axis=1, keepdims=True)
    high = combine.astype(jnp.bfloat16)
    low = (combine - high.astype(jnp.float32)).astype(jnp.bfloat16)
    grad_gates = jnp.zeros(combine.shape, jnp.float32)
    for t in range(3):
        cols, cols_up = slice(t * 256, t * 256 + 256), slice(WIDE + t * 256, WIDE + t * 256 + 256)
        gate = straight(x[...], gate_up[:, cols])
        up = straight(x[...], gate_up[:, cols_up])
        spread = straight(high, lanes[:, cols]) + straight(low, lanes[:, cols])
        grad_down = across(grads[:, :D], down[cols, :])
        sig = 1.0 / (1.0 + jnp.exp(-gate))
        silu = gate * sig
        inner = (silu * up).astype(jnp.bfloat16).astype(jnp.float32)
        inner_out[:, cols] = (inner * spread).astype(jnp.bfloat16)
        grad_inner = grad_down * spread
        acts_out[:, cols] = (grad_inner * up * sig * (1.0 + gate * (1.0 - sig))).astype(jnp.bfloat16)
        acts_out[:, cols_up] = (grad_inner * silu).astype(jnp.bfloat16)
        product = inner * grad_down
        product_high = product.astype(jnp.bfloat16)
        product_low = (product - product_high.astype(jnp.float32)).astype(jnp.bfloat16)
        grad_gates += across(product_high, lanes[:, cols]) + across(product_low, lanes[:, cols])
    grad_logits = combine * (grad_gates - jnp.sum(combine * grad_gates, axis=1, keepdims=True))
    logit_out[...] = grad_logits.astype(jnp.bfloat16)

    @pl.loop(0, 4)
    def _(k):
        back = across(acts_out[...], gate_up[cut(k, 256), :])
        back += across(logit_out[...], router[cut(k, 256), :])
        grad_x[:, cut(k, 256)] = back[:TOK_DEV].astype(jnp.bfloat16)
        grad_x_other[:, cut(k, 256)] = back[TOK_DEV:].astype(jnp.bfloat16)
        result = straight(inner_out[...], down[:, cut(k, 256)]).astype(jnp.bfloat16)
        mixed[:, cut(k, 256)] = result[:TOK_DEV]
        mixed_other[:, cut(k, 256)] = result[TOK_DEV:]


def hidden_grad_body(dy, hidden, cot, gain, valid, weight, grad_hidden, branch, grad_att, gain_grad):
    x, d = hidden[...], dy[...]
    scale = lax.rsqrt(jnp.mean(x * x, axis=1, keepdims=True) + epsilon)
    gain_grad[...] = jnp.sum(d * x * scale, axis=0, keepdims=True)
    g = d * gain[...]
    dx = scale * g - x * scale * scale * scale * jnp.mean(g * x, axis=1, keepdims=True)
    total = cot[...].astype(jnp.float32) + dx
    grad_hidden[...] = total
    branch[...] = (valid[...] * total).astype(jnp.bfloat16)

    @pl.loop(0, 4)
    def _(k):
        grad_att[:, cut(k, 256)] = across(branch[...], weight[cut(k, 256), :]).astype(jnp.bfloat16)


def attend_grad_body(
    tok, gain, cosine, sine_part, seg_col, seg_row, weight, turned, value, lse, grad_att, grad_hidden,
    grad_query, grad_key_value, grad_tok, gain_grad, grad_normed,
):
    bias = mask_bias(seg_col[...], seg_row[...])
    cos, sin = cosine[...], -sine_part[...]
    lane = lax.broadcasted_iota(jnp.int32, (TOK_DEV, 128), 1)

    @pl.loop(0, 4)
    def _(p):
        queries = turned[:, cut(p, 256)]
        keys = turned[:, pl.ds(pl.multiple_of(1024 + p * 128, 128), 128)]
        values = value[:, cut(p, 128)]
        grads = grad_att[:, cut(p, 256)]
        for_query, for_key, for_value = [], [0.0, 0.0], [0.0, 0.0]
        for h in range(4):
            side = slice(h // 2 * 64, h // 2 * 64 + 64)
            own = slice(h * 64, h * 64 + 64)
            log_total = jnp.sum(jnp.where(lane == p * 4 + h, lse[...], 0.0), axis=1, keepdims=True)
            prob = jnp.exp(across(queries[:, own], keys[:, side]) * SCORE_SCALE + bias - log_total)
            grad_prob = across(grads[:, own], values[:, side])
            for_value[h // 2] += down_rows(prob.astype(jnp.bfloat16), grads[:, own])
            row_dot = jnp.sum(prob * grad_prob, axis=1, keepdims=True)
            grad_scores = (prob * (grad_prob - row_dot)).astype(jnp.bfloat16)
            for_query.append(straight(grad_scores, keys[:, side]) * SCORE_SCALE)
            for_key[h // 2] += down_rows(grad_scores, queries[:, own]) * SCORE_SCALE
        q = jnp.concatenate(for_query, axis=1)
        q = jnp.concatenate([turn(q[:, :128], cos, sin), turn(q[:, 128:], cos, sin)], axis=1)
        grad_query[:, cut(p, 256)] = q.astype(jnp.bfloat16)
        k = turn(jnp.concatenate(for_key, axis=1), cos, sin)
        grad_key_value[:, cut(p, 128)] = k.astype(jnp.bfloat16)
        v = jnp.concatenate(for_value, axis=1)
        grad_key_value[:, pl.ds(pl.multiple_of(512 + p * 128, 128), 128)] = v.astype(jnp.bfloat16)

    @pl.loop(0, 4)
    def _(k):
        back = across(grad_query[...], weight[cut(k, 256), :D])
        grad_normed[:, cut(k, 256)] = back + across(grad_key_value[...], weight[cut(k, 256), D:])

    x, d = tok[...].astype(jnp.float32), grad_normed[...]
    scale = lax.rsqrt(jnp.mean(x * x, axis=1, keepdims=True) + epsilon)
    gain_grad[...] = jnp.sum(d * x * scale, axis=0, keepdims=True)
    g = d * gain[...]
    dx = scale * g - x * scale * scale * scale * jnp.mean(g * x, axis=1, keepdims=True)
    grad_tok[...] = (grad_hidden[...] + dx).astype(jnp.bfloat16)


def shards(
    tokens,
    sequence_lengths,
    expert_index,
    cotangent,
    query_weight,
    key_weight,
    value_weight,
    output_weight,
    attention_gain,
    router_weight,
    mixture_gain,
    gate_weight,
    up_weight,
    down_weight,
):
    bfloat = jnp.bfloat16
    single = jnp.float32
    c = lax.axis_index("core")
    small = jnp.concatenate(
        [router_weight, jnp.zeros((8, 114), bfloat), attention_gain[:, None], mixture_gain[:, None]], axis=1
    )
    attention_full = lax.all_gather(
        jnp.concatenate([query_weight, key_weight, value_weight, output_weight, small], axis=1),
        ALL, axis=0, tiled=True,
    )
    gains = attention_full[:, 3198:].astype(single).T
    attn_gain_full, mix_gain_full = gains[:1], gains[1:]

    segment, position, valid_slot = seq_layout(sequence_lengths[0])
    seg_col, seg_row = segment[:, None], segment[None, :]
    valid_rows = valid_slot.astype(single)[:, None]
    cosine, sine_part = rope_tables(position)
    pick = jnp.any(
        expert_index[:, :, None] == jnp.arange(128, dtype=jnp.int32)[None, None, :], axis=1
    ).astype(bfloat)
    early = group_gather(jnp.concatenate([cotangent * valid_rows.astype(bfloat), pick], axis=1))
    early = jnp.concatenate([early[i] for i in (4, 5, 2, 3, 6, 7, 0, 1)], axis=0)
    order = column_order().astype(bfloat)
    spread = spread_order().astype(bfloat)
    gate_up = jnp.concatenate([gate_weight, up_weight], axis=0).reshape(24 * 8, FF)
    gate_up = jnp.dot(gate_up, order, preferred_element_type=single).astype(bfloat)
    gate_up = gate_up.reshape(24, 8, 8, 64).transpose(2, 1, 0, 3).reshape(4, 2, 8, 2 * WIDE)
    gate_up = group_exchange(gate_up).reshape(128, WIDE)
    gate_up = jnp.dot(gate_up, spread, preferred_element_type=single).astype(bfloat).reshape(64, 2 * WIDE)
    share = jnp.concatenate([gate_up, down_packed(down_weight.reshape(1, 48, D))], axis=1)
    share = lax.all_gather(share, ("y", "x"), axis=0, tiled=True)
    down_full = down_unpacked(share[:, 2 * WIDE :])
    lanes = expert_lanes().astype(bfloat)

    normed_first, turned, value_rows, attended, lse, hidden, normed_second = kernel_call(
        attend_body,
        [
            ((256, D), bfloat), ((256, 1536), bfloat), ((256, 512), bfloat), ((256, D), bfloat),
            ((256, 128), single), ((256, D), single), ((256, D), bfloat),
        ],
        in_specs=[ALL_OF] * 8 + [QKV_PART, OUT_PART],
        flops=3 * 10**9, moved=20 * 10**6,
    )(
        tokens, attn_gain_full, mix_gain_full, cosine, sine_part, seg_col, seg_row, valid_rows,
        attention_full, attention_full,
    )

    saved = []

    def experts(k, block, block_other, after=()):
        outs = [
            ((2048, D), bfloat), ((2048, WIDE), bfloat), ((2048, 2 * WIDE), bfloat), ((2048, 128), bfloat),
        ] + [((256, D), bfloat)] * 4
        rows_of = lambda width: pl.BlockSpec((512, width), lambda i: (k, 0))
        specs = [ALL_OF, ALL_OF, rows_of(D + 128), ROUTER_PART, GATE_UP_PART, ALL_OF, ALL_OF]
        result = kernel_call(
            functools.partial(expert_body, len(after) + len(saved)),
            outs,
            in_specs=specs + [CORNER] * len(after) + [pl.BlockSpec(memory_space=pl.ANY)] * len(saved),
            out_specs=[rows_of(D), rows_of(WIDE), rows_of(2 * WIDE), rows_of(128)] + [ALL_OF] * 4,
            input_output_aliases={7 + len(after) + i: i for i in range(len(saved))},
            flops=20 * 10**9, moved=20 * 10**6,
        )(block, block_other, early, attention_full, share, down_full, lanes, *after, *saved)
        saved[:] = result[:4]
        mine, other, mine_mixed, other_mixed = result[4:]
        return add_low(mine, shift(other, "core", 1)), add_low(mine_mixed, shift(other_mixed, "core", 1))

    blocks = group_gather(normed_second)
    half = TOK_DEV // 2
    far, far_mixed = experts(0, blocks[4], blocks[5])
    near_below, mixed_below = experts(1, blocks[2], blocks[3])
    front, back = shift(far[:half], "z", 1), shift(far[half:], "z", -1)
    near_above, mixed_above = experts(2, blocks[6], blocks[7], [far])
    own, own_mixed = experts(3, blocks[0], blocks[1], [near_below])

    def with_far(below, above, front, back):
        below = jnp.concatenate([add_low(below[:half], front), below[half:]], axis=0)
        return below, jnp.concatenate([above[:half], add_low(above[half:], back)], axis=0)

    near_below, near_above = with_far(near_below, near_above, front, back)
    ahead, behind = shift(near_below, "z", 1), shift(near_above, "z", -1)
    rows, inner_scaled, grad_acts, grad_logits, _, _ = lax.optimization_barrier((*saved, near_below, near_above))
    grad_normed_second = sum(v.astype(single) for v in (own, ahead, behind))
    far_mixed, grad_normed_second = lax.optimization_barrier((far_mixed, grad_normed_second))
    front, back = shift(far_mixed[:half], "z", 1), shift(far_mixed[half:], "z", -1)

    grad_hidden, grad_branch, grad_attended, mixture_gain_grad = kernel_call(
        hidden_grad_body,
        [((256, D), single), ((256, D), bfloat), ((256, D), bfloat), ((1, D), single)],
        in_specs=[ALL_OF] * 5 + [OUT_PART],
        flops=10**9, moved=6 * 10**6,
    )(grad_normed_second, hidden, cotangent, mix_gain_full, valid_rows, attention_full)
    grad_query, grad_key_value, grad_tokens, attention_gain_grad = kernel_call(
        attend_grad_body,
        [((256, D), bfloat), ((256, D), bfloat), ((256, D), bfloat), ((1, D), single)],
        in_specs=[ALL_OF] * 6 + [QKV_PART] + [ALL_OF] * 5,
        scratch=[pltpu.VMEM((256, D), single)],
        flops=3 * 10**9, moved=12 * 10**6,
    )(
        tokens, attn_gain_full, cosine, sine_part, seg_col, seg_row, attention_full, turned, value_rows, lse,
        grad_attended, grad_hidden,
    )

    gate_up_grad = down_rows(rows, grad_acts).astype(bfloat)
    down_grad = down_rows(inner_scaled, early[:, :D]).astype(bfloat).reshape(16, 48, D)
    router_grad = down_rows(rows, grad_logits)
    owned = jnp.concatenate([gate_up_grad, down_packed(down_grad)], axis=1)
    owned = lax.psum_scatter(owned, ("y", "x"), scatter_dimension=0, tiled=True).astype(single)
    down_owned = down_unpacked(owned[:, 2 * WIDE :]).reshape(12, 4, D)
    owned = owned[:, : 2 * WIDE].reshape(128, WIDE)
    exact = lax.Precision.HIGHEST
    gathered = jnp.dot(owned, spread.T.astype(single), preferred_element_type=single, precision=exact)
    gathered = group_exchange(gathered.reshape(4, 2, 8, 2 * WIDE))

    normed_both = jnp.concatenate([normed_first, shift(normed_first, "core", 1)], axis=0)
    attended_both = jnp.concatenate([attended, shift(attended, "core", 1)], axis=0)

    def both_cores(left, right):
        mine, sent = jnp.where(c == 0, left, right), jnp.where(c == 0, right, left)
        return jnp.concatenate([mine, shift(sent, "core", 1)], axis=0)

    branch_both = both_cores(grad_branch[:, : D // 2], grad_branch[:, D // 2 :])
    output_grad = down_rows(attended_both, branch_both).astype(bfloat)
    qkv_both = both_cores(grad_query, grad_key_value)
    qkv_grad = down_rows(normed_both, qkv_both).astype(bfloat)
    small_grad = jnp.concatenate(
        [router_grad[:, :126], attention_gain_grad.T, mixture_gain_grad.T], axis=1
    ).astype(bfloat)
    small_grad = add_low(small_grad, shift(small_grad, "core", 1))
    first = torus_sum(qkv_grad[:, :768].reshape(4, 4, 4, 16, 768), "yxz", "yxz", direct_sum)
    second = jnp.concatenate([qkv_grad[:, 768:], small_grad, output_grad], axis=1)
    second = torus_sum(second.reshape(4, 4, 4, 16, 896), "x", "yxz", direct_sum).astype(bfloat)
    second, front, back = lax.optimization_barrier((second, front, back))
    mixed_below, mixed_above = with_far(mixed_below, mixed_above, front, back)
    mixed_ahead, mixed_behind = shift(mixed_below, "z", 1), shift(mixed_above, "z", -1)
    mixture = sum(v.astype(single) for v in (own_mixed, mixed_ahead, mixed_behind))
    layer_out = (hidden + valid_rows * mixture).astype(bfloat)
    second = torus_sum(second, "y", "yz", direct_sum).astype(bfloat)
    second, gathered, layer_out = lax.optimization_barrier((second, gathered, layer_out))
    second = torus_sum(second, "z", "z", direct_sum)
    owned = gathered.reshape(8, 8, 24, 64).transpose(2, 1, 0, 3).reshape(24 * 8, FF)
    owned = jnp.dot(owned, order.T.astype(single), preferred_element_type=single, precision=exact)
    owned = owned.reshape(2, EXPERTS, 8, FF)
    gate_owned, up_owned = owned[0], owned[1]
    half = jnp.concatenate([first, second], axis=1)
    mine = lax.dynamic_slice_in_dim(half, c * 8, 8, axis=0)
    got = shift(lax.dynamic_slice_in_dim(half, (1 - c) * 8, 8, axis=0), "core", 1)
    left, right = jnp.where(c == 0, mine, got), jnp.where(c == 0, got, mine)
    return (
        layer_out,
        grad_tokens,
        left[:, :D],
        right[:, :512],
        right[:, 512:D],
        jnp.concatenate([left[:, 1152:], right[:, 1152:]], axis=1),
        left[:, 1150],
        left[:, 1024:1036],
        left[:, 1151],
        gate_owned,
        up_owned,
        down_owned,
    )


def solution(mesh):
    mesh = Mesh(mesh.devices.reshape(4, 4, 4, 2), ALL)
    rows, line, inner = P(ALL, None), P(ALL), P(None, ALL, None)
    return jax.shard_map(
        shards,
        mesh=mesh,
        in_specs=(rows,) * 8 + (line, rows, line) + (inner,) * 3,
        out_specs=(rows,) * 6 + (line, rows, line) + (inner,) * 3,
        check_vma=False,
    )
```
